32 devices in a mesh: group: 2 (over y), tile: 4 (over z), strip: 2 (over x), sub: 2 (over core).
Axes of the slice: x: 2, y: 2, z: 4, core: 2. Of those that a mesh axis runs over, the one named last changes fastest.
Arguments:
- right_side: float32 [32, 128, 1024], P('group', 'tile', ('strip', 'sub')), parts along dimension 0, may hold values from -24 to 24
- horiz_coef: float32 [256, 1024], P(('group', 'tile'), ('strip', 'sub')), parts along dimension 0, may hold values from 8 to 32
- vert_coef: float32 [256, 1024], P(('group', 'tile'), ('strip', 'sub')), parts along dimension 0, may hold values from 1 to 8
- panel_owner: int32 [16384, 1], P(('group', 'tile', 'strip', 'sub')), parts along dimension 0, may hold values from 0 to 3; in each aligned block of 512 rows (0 to 511, 512 to 1023, ...) at most 384 rows name the same one
- panel_cell: int32 [16384], P(('group', 'tile', 'strip', 'sub')), parts along dimension 0, may hold values from 0 to 8191
- panel_pressure: float32 [16384], P(('group', 'tile', 'strip', 'sub')), parts along dimension 0, may hold values from -48 to 48
Outputs:
- potential: float32 [32, 128, 1024], P('group', 'tile', ('strip', 'sub')), parts along dimension 0
- residual: float32 [32, 128, 1024], P('group', 'tile', ('strip', 'sub')), parts along dimension 0
The draws below stay inside these ranges and needn't reach their ends.
There are 2 independent parts, one for each index of `group`. The reference program is written for one: setup_inputs(seed, part) draws one part's arguments, and reference() takes and returns one part's arrays. A program takes and returns all parts, laid end to end along the dimension named above; each array names one. Nothing has to cross between parts.
Inputs may be any that keep to these rules, and one draw needn't show every extreme that they name: `panel_owner`: among the 512 panels of one device at most 384 name one owner; some device reaches 384 in every draw.
All inputs are finite; a program needn't handle non-finite values.
Results may differ from the reference program's by a relative error of at most 0.00015.
Values sent between devices are 32-bit elements; how exact they have to be, the bound alone decides.
A program may use at most 128 MiB of HBM per device.

```python
import math
import jax
import jax.numpy as jnp
import numpy as np
from jax import lax

NZ = 16
CX = 32
CY = 256
LEVELS = 3
SWEEPS = 2
COARSE = 8
PAN_DEV = 512
TILES = 4
CAP = 384
NX = 128
NY = 1024
PANELS = 8192


def touch_ends(result, rng, least, top_value):
    longest = result.shape.index(max(result.shape))
    spots = []
    for shift in (0, 1):
        where = [jax.random.randint(jax.random.fold_in(rng, axis), (), 0, length) for axis, length in enumerate(result.shape)]
        where[longest] = (where[longest] + shift) % result.shape[longest]
        spots.append(tuple(where))
    return result.at[spots[0]].set(least).at[spots[1]].set(top_value)


def level_of(rng, extent, split, least, high):
    loudness, own = 1.0, jax.random.fold_in(rng, 6)
    for position, blocks in split:
        heights = jnp.exp(jax.random.uniform(jax.random.fold_in(own, position), (blocks,), jnp.float32, least / len(split), high / len(split)))
        loudness = loudness * jnp.repeat(heights, extent[position] // blocks).reshape([-1 if axis == position else 1 for axis in range(len(extent))])
    return loudness


def routed_block(key, own, number, rows, number_of, top, reach, lean):
    ranking = jax.random.permutation(key, number_of)
    packed, usual = load_shares(number_of, rows * top, reach, lean, True), load_shares(number_of, rows * top, reach, lean, False)
    places = jnp.arange(number_of)

    def named(sizes, offset_by):
        used = int((sizes > 0).sum())
        fixed = max(1, used // 4)
        passed = fixed + (places - fixed + offset_by * (used - fixed)) % max(1, number_of - fixed)
        return jnp.zeros((number_of,), jnp.int32).at[ranking[jnp.where(places < fixed, places, passed)]].set(jnp.asarray(sizes, jnp.int32))

    sizes = jnp.where(number % 4 == 0, named(packed, number // 4), named(usual, number - number // 4 - 1))
    mixed = jax.random.permutation(jax.random.fold_in(own, 3), number_of)
    source_of, receiver = mixed[0:number_of // 2 * 2:2], mixed[1:number_of // 2 * 2:2]
    slack = jnp.minimum(sizes[source_of] - 1, reach - sizes[receiver]) // 2
    slack = jnp.where((source_of == ranking[0]) | (receiver == ranking[0]) | (sizes[receiver] == 0), 0, jnp.maximum(slack, 0))
    passed = jax.random.randint(jax.random.fold_in(own, 4), (number_of // 2,), 0, 1 << 20) % (slack + 1)
    sizes = sizes.at[source_of].add(-passed).at[receiver].add(passed)
    items = jnp.searchsorted(jnp.cumsum(sizes), jnp.arange(rows * top), side="right").astype(jnp.int32)
    listing = items.reshape(top, rows).T
    listing = listing[jax.random.permutation(jax.random.fold_in(own, 1), rows)]
    offset_by = jax.random.randint(jax.random.fold_in(own, 2), (rows, 1), 0, top)
    return jnp.take_along_axis(listing, (jnp.arange(top)[None, :] + offset_by) % top, axis=1)


def load_shares(number_of, total, most, skew, full):
    loads = [(1 << 20) // math.isqrt(standing ** skew) + 1 for standing in range(1, number_of + 1)]
    largest = most if full else min(most, max(-(-total // number_of), total * loads[0] // sum(loads)))
    least = 1 if total - largest >= number_of - 1 else 0
    holding, surplus = [largest] + [least] * (number_of - 1), total - largest - least * (number_of - 1)
    while surplus > 0:
        free = [i for i in range(1, number_of) if holding[i] < largest] or [i for i in range(1, number_of) if holding[i] < most]
        whole, left = sum([loads[i] for i in free]), surplus
        for i in free:
            extra = min(most - holding[i], max(1, left * loads[i] // whole), surplus)
            holding[i] = holding[i] + extra
            surplus = surplus - extra
    return np.array(holding)


def noise(rng, shape, deviation, reach, pieces=(), kind=jnp.bfloat16):
    drawn = deviation * jax.random.normal(rng, shape, jnp.float32)
    if pieces:
        drawn = drawn * level_of(rng, shape, pieces, -0.22, 0.18)
    return jnp.clip(drawn, -reach, reach).astype(kind)


def setup_inputs(seed: int = 0, part: int = 0) -> dict:
    seeds = jax.random.split(jax.random.key(seed), 7)
    part_keys = jax.random.split(jax.random.fold_in(seeds[6], part), 7)
    right_side = noise(part_keys[0], (NZ, NX, NY), 4.0, 24.0, ((1, 4), (2, 4)), jnp.float32)
    horiz_coef = jnp.clip(jnp.exp(math.log(32.0) - 1.3862944 * jax.random.uniform(part_keys[1], (NX, NY), jnp.float32) ** level_of(part_keys[1], (NX, NY), ((0, 4), (1, 4)), -0.2, 0.2)), 8.0, 32.0)
    vert_coef = jnp.clip(jnp.exp(math.log(8.0) - 2.0794415 * jax.random.uniform(part_keys[2], (NX, NY), jnp.float32) ** level_of(part_keys[2], (NX, NY), ((0, 4), (1, 4)), -0.2, 0.2)), 1.0, 8.0)
    panel_owner_keys = jax.random.split(jax.random.fold_in(part_keys[3], 1), PANELS // PAN_DEV)
    panel_owner_turns = jax.random.permutation(jax.random.fold_in(part_keys[3], 3), PANELS // PAN_DEV)
    panel_owner = jax.vmap(lambda own, number: routed_block(jax.random.fold_in(part_keys[3], 2), own, number, PAN_DEV, TILES, 1, CAP, 2))(panel_owner_keys, panel_owner_turns).reshape((PANELS, 1))
    panel_cell = touch_ends(jax.random.randint(part_keys[4], (PANELS,), 0, CX * CY), jax.random.fold_in(part_keys[4], 1), 0, (CX * CY) - 1).astype(jnp.int32)
    panel_pressure = noise(part_keys[5], (PANELS,), 8.0, 48.0, ((0, 16),), jnp.float32)
    return {"right_side": right_side, "horiz_coef": horiz_coef, "vert_coef": vert_coef, "panel_owner": panel_owner, "panel_cell": panel_cell, "panel_pressure": panel_pressure}


OMEGA = 0.8


def diag_of(kh, kv, scale, depth):
    lower = (lax.iota(jnp.int32, depth) > 0).astype(kh.dtype)
    return 4.0 * scale * kh[None] + kv[None] * (1.0 + lower[:, None, None])


def apply_level(field, kh, kv, scale):
    padded = jnp.pad(field, ((0, 0), (1, 1), (1, 1)))
    hsum = padded[:, 2:, 1:-1] + padded[:, :-2, 1:-1] + padded[:, 1:-1, 2:] + padded[:, 1:-1, :-2]
    zeros = jnp.zeros_like(field[:1])
    above = jnp.concatenate([field[1:], zeros], 0)
    below = jnp.concatenate([zeros, field[:-1]], 0)
    diag = diag_of(kh, kv, scale, field.shape[0])
    return diag * field - scale * kh[None] * hsum - kv[None] * (above + below)


def relax_from(field, source, kh, kv, scale, count):
    diag = diag_of(kh, kv, scale, source.shape[0])
    for step in range(count):
        field = field + OMEGA * (source - apply_level(field, kh, kv, scale)) / diag
    return field


def coarsen(field):
    shape = field.shape
    return field.reshape(shape[:-2] + (shape[-2] // 2, 2, shape[-1] // 2, 2)).mean(axis=(-3, -1))


def cycle(source, kh, kv, level):
    scale = 0.25 ** level
    diag = diag_of(kh, kv, scale, source.shape[0])
    first = OMEGA * source / diag
    if level == LEVELS - 1:
        return relax_from(first, source, kh, kv, scale, COARSE - 1)
    field = relax_from(first, source, kh, kv, scale, SWEEPS - 1)
    remain = source - apply_level(field, kh, kv, scale)
    correction = cycle(coarsen(remain), coarsen(kh), coarsen(kv), level + 1)
    field = field + jnp.repeat(jnp.repeat(correction, 2, axis=1), 2, axis=2)
    return relax_from(field, source, kh, kv, scale, SWEEPS)


def reference(right_side, horiz_coef, vert_coef, panel_owner, panel_cell, panel_pressure):
    block = jnp.arange(PANELS, dtype=jnp.int32) // PAN_DEV
    column = block % (NY // CY)
    gx = panel_owner[:, 0] * CX + panel_cell // CY
    gy = column * CY + panel_cell % CY
    forcing = jnp.zeros((NX, NY), jnp.float32).at[gx, gy].add(panel_pressure)
    source = right_side.at[NZ - 1].add(forcing)
    potential = cycle(source, horiz_coef, vert_coef, 0)
    residual = source - apply_level(potential, horiz_coef, vert_coef, 1.0)
    return potential, residual
```

```python
import functools

import jax
import jax.numpy as jnp
from jax import lax
from jax.experimental import pallas as pl
from jax.experimental.pallas import tpu as pltpu
from jax.sharding import PartitionSpec as P

MESH = pl.DeviceIdType.MESH
OMEGA = 0.8
NZ = 16
ND = 24
SLOT = 16
HALO = (4, 5, 9)
REACH = (1, 1, 2)


def split3(x):
    a = x.astype(jnp.bfloat16)
    y = x - a.astype(jnp.float32)
    b = y.astype(jnp.bfloat16)
    c = (y - b.astype(jnp.float32)).astype(jnp.bfloat16)
    return a, b, c


def dot3(x, m):
    out = None
    for part in split3(x):
        d = jnp.dot(part, m, preferred_element_type=jnp.float32)
        out = d if out is None else out + d
    return out


def down_matrix(rows, cols):
    i = lax.broadcasted_iota(jnp.int32, (rows, cols), 0)
    j = lax.broadcasted_iota(jnp.int32, (rows, cols), 1)
    return jnp.where((i == 2 * j) | (i == 2 * j + 1), 1.0, 0.0).astype(jnp.bfloat16)


def up_matrix(rows, cols, local):
    i = lax.broadcasted_iota(jnp.int32, (rows, cols), 0)
    j = lax.broadcasted_iota(jnp.int32, (rows, cols), 1)
    right = (2 * i == j) | (2 * i + 1 == j)
    ib, jb = 2 * (i - rows), j - cols
    left = (ib == jb) | (ib + 1 == jb)
    hit = ((j < local + 64) & right) | ((j >= local + 64) & left)
    return jnp.where(hit, 1.0, 0.0).astype(jnp.bfloat16)


def kernel(
    dims, rs, kh, kv, owner, cell, pressure, pot, res,
    fpart, frecv, stack, e0, e1, e2, ua0, ub0, rd0, ua1, ub1, rd1, ua2, ub2, rd2,
    t0, t1, rfine, ps0, ps1, ps2, pr0, pr1, pr2, fs_sem, fr_sem, ss, rsem,
):
    tiles, columns, subs = dims
    nx, ny = rs.shape[1], rs.shape[2]
    sizes = (nx, nx // 2, nx // 4)
    widths = (ny, ny // 2, ny // 4)
    es, pss, prs = (e0, e1, e2), (ps0, ps1, ps2), (pr0, pr1, pr2)
    me = lax.axis_index("tile")
    col = lax.axis_index("strip") * subs + lax.axis_index("sub")

    def device(dt, dc):
        c = col + dc
        return {"tile": me + dt, "strip": c // subs, "sub": c % subs}

    def exists(dt, dc):
        ok = jnp.bool_(True)
        if dt:
            t = me + dt
            ok = ok & (t >= 0) & (t < tiles)
        if dc:
            c = col + dc
            ok = ok & (c >= 0) & (c < columns)
        return ok

    for ref in (e0, e1, e2, pr0, pr1, pr2):
        ref[...] = jnp.zeros_like(ref)

    barrier = pltpu.get_barrier_semaphore()
    near = [(dt, dc) for dt in range(-2, 3) for dc in (-1, 0, 1) if dc]
    expected = jnp.int32(tiles - 1)
    for k in range(1, tiles):
        pl.semaphore_signal(barrier, inc=1, device_id={"tile": (me + k) % tiles}, device_id_type=MESH)
    for dt, dc in near:
        ok = exists(dt, dc)
        expected = expected + ok.astype(jnp.int32)

        @pl.when(ok)
        def _():
            pl.semaphore_signal(barrier, inc=1, device_id=device(dt, dc), device_id_type=MESH)

    for ref in (ua0, ub0, ua1, ub1, ua2, ub2):
        ref[...] = jnp.zeros_like(ref)

    g = owner[...] * nx + cell[...] // ny
    y = cell[...] % ny
    parts = split3(pressure[...])
    left, right = [], []
    q = g.shape[0]
    ix = lax.broadcasted_iota(jnp.int32, (tiles * nx, 128), 0)
    iy = lax.broadcasted_iota(jnp.int32, (ny, 128), 0)
    for k in range(q):
        hit = ix == g[k:k + 1]
        left.append(jnp.concatenate(
            [jnp.where(hit, p.astype(jnp.float32)[k:k + 1], 0.0).astype(jnp.bfloat16) for p in parts], 0))
        right.append(jnp.where(iy == y[k:k + 1], 1.0, 0.0).astype(jnp.bfloat16))
    f3 = lax.dot_general(jnp.concatenate(left, 1), jnp.concatenate(right, 1), (((1,), (1,)), ((), ())),
                         preferred_element_type=jnp.float32)
    n = tiles * nx
    fpart[...] = (f3[:n] + f3[n:2 * n] + f3[2 * n:]).reshape(tiles, nx, ny)

    pl.semaphore_wait(barrier, expected)

    copies = []
    for k in range(1, tiles):
        to = (me + k) % tiles
        c = pltpu.make_async_remote_copy(
            src_ref=fpart.at[to], dst_ref=frecv.at[k - 1], send_sem=fs_sem.at[k - 1],
            recv_sem=fr_sem.at[k - 1], device_id={"tile": to}, device_id_type=MESH)
        c.start()
        copies.append(c)
    stack[0:NZ] = rs[...]
    stack[NZ] = kh[...]
    stack[NZ + 1] = kv[...]
    for k in range(NZ + 2, ND):
        stack[k] = jnp.zeros((nx, ny), jnp.float32)
    for c in copies:
        c.wait()
    force = fpart[me]
    for k in range(tiles - 1):
        force = force + frecv[k]
    stack[NZ - 1] = rs[NZ - 1] + force
    h0 = HALO[0]
    e0[h0:h0 + nx, :, 0:ny] = jnp.swapaxes(stack[...], 0, 1)

    lane = lax.broadcasted_iota(jnp.int32, (1, 128), 1)

    def exchange(level):
        e, ps, pr, h, n, w = es[level], pss[level], prs[level], HALO[level], sizes[level], widths[level]
        wt = e.shape[2]
        npk = n // 8
        edge = ((0, 0), ((w - 1) // 128 * 128, (w - SLOT) % 128))
        for side in (0, 1):
            base, off = edge[side]
            for k in range(npk):
                acc = None
                for j in range(8):
                    v = e[h + 8 * k + j, :, base:base + 128]
                    shift = (SLOT * j - off) % 128
                    v = pltpu.roll(v, shift, 1) if shift else v
                    acc = v if acc is None else jnp.where(lane >= SLOT * j, v, acc)
                ps[side, k] = acc
        index = 0
        pending = []
        for dt in range(-REACH[level], REACH[level] + 1):
            for dc in (-1, 0, 1):
                if not (dt or dc):
                    continue
                d = abs(dt)
                if dc == 0:
                    m = min(n, h - (d - 1) * n)
                    send_lo = h if dt < 0 else h + n - m
                    land = h + d * n if dt < 0 else h - (d - 1) * n - m
                    lanes = pl.ds(0, max(w, 128))
                    src = e.at[pl.ds(send_lo, m), :, lanes]
                    dst = e.at[pl.ds(land, m), :, lanes]
                else:
                    side = 0 if dc < 0 else 1
                    slot = (-dt + REACH[level]) * 2 + (1 if dc < 0 else 0)
                    if dt == 0:
                        src, dst = ps.at[side], pr.at[slot]
                    else:
                        k = 0 if dt < 0 else npk - 1
                        src, dst = ps.at[side, pl.ds(k, 1)], pr.at[slot, pl.ds(0, 1)]
                c = pltpu.make_async_remote_copy(
                    src_ref=src, dst_ref=dst, send_sem=ss.at[level, index], recv_sem=rsem.at[level, index],
                    device_id=device(dt, dc), device_id_type=MESH)
                pending.append((c, exists(dt, dc), exists(-dt, -dc)))
                index += 1
        for c, to, _ in pending:
            pl.when(to)(c.start)
        for c, to, _ in pending:
            pl.when(to)(c.wait_send)
        for c, _, come in pending:
            pl.when(come)(c.wait_recv)
        rbase, roff = w // 128 * 128, w % 128
        hb = wt - 128

        def put(row, dt, k, j):
            slot = (dt + REACH[level]) * 2
            from_left = pr[slot, k]
            from_right = pr[slot + 1, k]
            s1 = (128 - SLOT - SLOT * j) % 128
            s2 = (roff - SLOT * j) % 128
            from_left = pltpu.roll(from_left, s1, 1) if s1 else from_left
            from_right = pltpu.roll(from_right, s2, 1) if s2 else from_right
            own = e[row, :, hb:hb + 128] if roff else jnp.zeros((ND, 128), jnp.float32)
            inner = jnp.where((lane >= roff) & (lane < roff + SLOT), from_right, own)
            e[row, :, hb:hb + 128] = jnp.where(lane >= 128 - SLOT, from_left, inner)

        for r in range(n):
            put(h + r, 0, r // 8, r % 8)
        for d in range(1, REACH[level] + 1):
            m = min(n, h - (d - 1) * n)
            for r in range(m):
                put(h - (d - 1) * n - m + r, -d, 0, (n - m + r) % 8)
                put(h + d * n + r, d, 0, r % 8)

    z = lax.broadcasted_iota(jnp.int32, (1, NZ, 1), 1)

    def diag_of(k_h, k_v):
        return 4.0 * k_h + k_v * jnp.where(z > 0, 2.0, 1.0)

    def coefs(e, r, count, scale):
        return scale * e[pl.ds(r, count), NZ:NZ + 1, :], e[pl.ds(r, count), NZ + 1:NZ + 2, :]

    def over(lo, hi, step, fn):
        def loop(i, carry):
            fn(lo + i * step)
            return carry
        lax.fori_loop(0, (hi - lo) // step, loop, 0)

    def first(e, rd, u, scale, rows):
        def at(r):
            k_h, k_v = coefs(e, r, 2, scale)
            diag = diag_of(k_h, k_v)
            inv = jnp.where(diag > 0.0, OMEGA / diag, 0.0)
            rd[pl.ds(r, 2)] = inv
            u[pl.ds(r + 1, 2)] = inv * e[pl.ds(r, 2), 0:NZ, :]
        over(0, rows, 2, at)

    def terms(e, u, r, count, scale):
        wt = u.shape[2]
        k_h, k_v = coefs(e, r, count, scale)
        x = u[pl.ds(r + 1, count)]
        hs = u[pl.ds(r, count)] + u[pl.ds(r + 2, count)]
        hs = hs + pltpu.roll(x, 1, 2) + pltpu.roll(x, wt - 1, 2)
        vs = jnp.where(z < NZ - 1, pltpu.roll(x, NZ - 1, 1), 0.0) + jnp.where(z > 0, pltpu.roll(x, 1, 1), 0.0)
        return x, e[pl.ds(r, count), 0:NZ, :] + k_h * hs + k_v * vs, k_h, k_v

    def sweep(e, rd, u, v, scale, rows):
        def at(r):
            x, t, _, _ = terms(e, u, r, 2, scale)
            v[pl.ds(r + 1, 2)] = (1.0 - OMEGA) * x + rd[pl.ds(r, 2)] * t
        over(0, rows, 2, at)

    def residue(e, u, r, count, scale):
        x, t, k_h, k_v = terms(e, u, r, count, scale)
        return t - diag_of(k_h, k_v) * x

    def restrict(level, u, t):
        e, h, n, w = es[level], HALO[level], sizes[level], widths[level]
        scale = 0.25 ** level
        wt = t.shape[2]

        def at(k):
            r = h + 2 * k
            both = residue(e, u, r, 2, scale)[:, :, 0:wt]
            t[k, 0:NZ] = 0.25 * (both[0] + both[1])
            t[k, NZ:ND] = 0.25 * (e[r, NZ:ND, 0:wt] + e[r + 1, NZ:ND, 0:wt])
        over(0, n // 2, 1, at)
        out = dot3(t[...].reshape(n // 2 * ND, wt), down_matrix(wt, 128))
        if w // 2 < 128:
            out = jnp.where(lane < w // 2, out, 0.0)
        es[level + 1][pl.ds(HALO[level + 1], n // 2), :, 0:128] = out.reshape(n // 2, ND, 128)

    def prolong(level, u, lo, count, fine, fine_lo):
        wt, wf = u.shape[2], fine.shape[2]
        m = up_matrix(wt, wf, widths[level - 1])
        rows = dot3(u[lo + 1:lo + 1 + count].reshape(count * NZ, wt), m).reshape(count, NZ, wf)
        for k in range(count):
            for j in range(2):
                f = fine_lo + 1 + 2 * k + j
                fine[f] = fine[f] + rows[k]

    n0, n1, n2 = (sizes[k] + 2 * HALO[k] for k in range(3))
    exchange(0)
    first(e0, rd0, ua0, 1.0, n0)
    sweep(e0, rd0, ua0, ub0, 1.0, n0)
    restrict(0, ub0, t0)
    exchange(1)
    first(e1, rd1, ua1, 0.25, n1)
    sweep(e1, rd1, ua1, ub1, 0.25, n1)
    restrict(1, ub1, t1)
    exchange(2)
    first(e2, rd2, ua2, 0.0625, n2)
    for _ in range(3):
        sweep(e2, rd2, ua2, ub2, 0.0625, n2)
        sweep(e2, rd2, ub2, ua2, 0.0625, n2)
    sweep(e2, rd2, ua2, ub2, 0.0625, n2)
    prolong(2, ub2, HALO[2] - 2, sizes[2] + 4, ub1, HALO[1] - 4)
    sweep(e1, rd1, ub1, ua1, 0.25, n1)
    sweep(e1, rd1, ua1, ub1, 0.25, n1)
    prolong(1, ub1, HALO[1] - 2, sizes[1] + 4, ub0, 0)
    sweep(e0, rd0, ub0, ua0, 1.0, n0)
    sweep(e0, rd0, ua0, ub0, 1.0, n0)

    def last(k):
        rfine[pl.ds(k, 2)] = residue(e0, ub0, h0 + k, 2, 1.0)[:, :, 0:ny]
    over(0, nx, 2, last)
    pot[...] = jnp.swapaxes(ub0[h0 + 1:h0 + 1 + nx, :, 0:ny], 0, 1)
    res[...] = jnp.swapaxes(rfine[...], 0, 1)


def solution(mesh):
    tiles, strips, subs = mesh.shape["tile"], mesh.shape["strip"], mesh.shape["sub"]

    def body(right_side, horiz_coef, vert_coef, panel_owner, panel_cell, panel_pressure):
        nz, nx, ny = right_side.shape
        rows = [n + 2 * h for n, h in zip((nx, nx // 2, nx // 4), HALO)]
        wts = (ny + 128, ny // 2 + 128, 128)
        f32 = jnp.float32
        scratch = [
            pltpu.VMEM((tiles, nx, ny), f32),
            pltpu.VMEM((max(tiles - 1, 1), nx, ny), f32),
            pltpu.VMEM((ND, nx, ny), f32),
        ]
        scratch += [pltpu.VMEM((rows[k], ND, wts[k]), f32) for k in range(3)]
        for k in range(3):
            scratch += [pltpu.VMEM((rows[k] + 2, NZ, wts[k]), f32)] * 2 + [pltpu.VMEM((rows[k], NZ, wts[k]), f32)]
        scratch += [pltpu.VMEM((nx // 2, ND, ny), f32), pltpu.VMEM((nx // 4, ND, ny // 2), f32)]
        scratch += [pltpu.VMEM((nx, NZ, ny), f32)]
        scratch += [pltpu.VMEM((2, nx // 8 >> k, ND, 128), f32) for k in range(3)]
        scratch += [pltpu.VMEM((2 * (2 * REACH[k] + 1), nx // 8 >> k, ND, 128), f32) for k in range(3)]
        scratch += [
            pltpu.SemaphoreType.DMA((max(tiles - 1, 1),)),
            pltpu.SemaphoreType.DMA((max(tiles - 1, 1),)),
            pltpu.SemaphoreType.DMA((3, 14)),
            pltpu.SemaphoreType.DMA((3, 14)),
        ]
        panels = panel_cell.shape[0]
        out = jax.ShapeDtypeStruct((nz, nx, ny), f32)
        vmem = pl.BlockSpec(memory_space=pltpu.VMEM)
        return pl.pallas_call(
            functools.partial(kernel, (tiles, strips * subs, subs)),
            out_shape=(out, out),
            in_specs=[vmem] * 6,
            out_specs=(vmem, vmem),
            scratch_shapes=scratch,
            compiler_params=pltpu.CompilerParams(
                collective_id=0, has_side_effects=True, vmem_limit_bytes=40 * 1024 * 1024
            ),
        )(
            right_side, horiz_coef, vert_coef,
            panel_owner.reshape(panels // 128, 128), panel_cell.reshape(panels // 128, 128),
            panel_pressure.reshape(panels // 128, 128),
        )

    return jax.shard_map(
        body,
        mesh=mesh,
        in_specs=(
            P("group", "tile", ("strip", "sub")),
            P(("group", "tile"), ("strip", "sub")),
            P(("group", "tile"), ("strip", "sub")),
            P(("group", "tile", "strip", "sub"), None),
            P(("group", "tile", "strip", "sub")),
            P(("group", "tile", "strip", "sub")),
        ),
        out_specs=(P("group", "tile", ("strip", "sub")), P("group", "tile", ("strip", "sub"))),
        check_vma=False,
    )
```

```python
import functools

import jax
import jax.numpy as jnp
from jax import lax
from jax.experimental import pallas as pl
from jax.experimental.pallas import tpu as pltpu
from jax.sharding import PartitionSpec as P

MESH = pl.DeviceIdType.MESH
OMEGA = 0.8
NZ = 16
ND = 24
SLOT = 16
HALO = (4, 5, 9)
REACH = (1, 1, 2)
BLOCK = (8, 12, 26)


def split3(x):
    a = x.astype(jnp.bfloat16)
    y = x - a.astype(jnp.float32)
    b = y.astype(jnp.bfloat16)
    c = (y - b.astype(jnp.float32)).astype(jnp.bfloat16)
    return a, b, c


def dot3(x, m):
    out = None
    for part in split3(x):
        d = jnp.dot(part, m, preferred_element_type=jnp.float32)
        out = d if out is None else out + d
    return out


def down_matrix(rows, cols):
    i = lax.broadcasted_iota(jnp.int32, (rows, cols), 0)
    j = lax.broadcasted_iota(jnp.int32, (rows, cols), 1)
    return jnp.where((i == 2 * j) | (i == 2 * j + 1), 1.0, 0.0).astype(jnp.bfloat16)


def up_matrix(rows, cols, local):
    i = lax.broadcasted_iota(jnp.int32, (rows, cols), 0)
    j = lax.broadcasted_iota(jnp.int32, (rows, cols), 1)
    right = (2 * i == j) | (2 * i + 1 == j)
    ib, jb = 2 * (i - rows), j - cols
    left = (ib == jb) | (ib + 1 == jb)
    hit = ((j < local + 64) & right) | ((j >= local + 64) & left)
    return jnp.where(hit, 1.0, 0.0).astype(jnp.bfloat16)


def kernel(
    dims, rs, kh, kv, owner_in, cell_in, pressure_in, pot, res,
    fpart, frecv, stack, e0, e1, e2, ua0, ub0, rd0, ua1, ub1, rd1, ua2, ub2, rd2,
    t0, t1, rfine, ps0, ps1, ps2, pr0, pr1, pr2, owner, cell, pressure,
    fs_sem, fr_sem, ss, rsem, in_sem,
):
    tiles, columns, subs = dims
    nx, ny = rs.shape[1], rs.shape[2]
    sizes = (nx, nx // 2, nx // 4)
    widths = (ny, ny // 2, ny // 4)
    es, pss, prs = (e0, e1, e2), (ps0, ps1, ps2), (pr0, pr1, pr2)
    me = lax.axis_index("tile")
    col = lax.axis_index("strip") * subs + lax.axis_index("sub")

    def device(dt, dc):
        c = col + dc
        return {"tile": me + dt, "strip": c // subs, "sub": c % subs}

    def exists(dt, dc):
        ok = jnp.bool_(True)
        if dt:
            t = me + dt
            ok = ok & (t >= 0) & (t < tiles)
        if dc:
            c = col + dc
            ok = ok & (c >= 0) & (c < columns)
        return ok

    loads = [
        pltpu.make_async_copy(src, dst, in_sem.at[k])
        for k, (src, dst) in enumerate((
            (owner_in, owner), (cell_in, cell), (pressure_in, pressure),
            (rs, stack.at[pl.ds(0, NZ)]), (kh, stack.at[NZ]), (kv, stack.at[NZ + 1])))
    ]
    for c in loads:
        c.start()
    for level in range(3):
        e, h, n = es[level], HALO[level], sizes[level]
        wt = e.shape[2]
        e[0:h] = jnp.zeros((h, ND, wt), jnp.float32)
        e[h + n:] = jnp.zeros((h, ND, wt), jnp.float32)
        prs[level][...] = jnp.zeros_like(prs[level])

    barrier = pltpu.get_barrier_semaphore()
    near = [(dt, dc) for dt in range(-2, 3) for dc in (-1, 0, 1) if dc]
    expected = jnp.int32(tiles - 1)
    for k in range(1, tiles):
        pl.semaphore_signal(barrier, inc=1, device_id={"tile": (me + k) % tiles}, device_id_type=MESH)
    for dt, dc in near:
        ok = exists(dt, dc)
        expected = expected + ok.astype(jnp.int32)

        @pl.when(ok)
        def _():
            pl.semaphore_signal(barrier, inc=1, device_id=device(dt, dc), device_id_type=MESH)

    for ref in (ua0, ub0, ua1, ub1, ua2, ub2):
        ref[0] = jnp.zeros(ref.shape[1:], jnp.float32)
        ref[ref.shape[0] - 1] = jnp.zeros(ref.shape[1:], jnp.float32)
    for c in loads[:3]:
        c.wait()

    g = owner[...] * nx + cell[...] // ny
    y = cell[...] % ny
    parts = split3(pressure[...])
    left, right = [], []
    q = g.shape[0]
    ix = lax.broadcasted_iota(jnp.int32, (tiles * nx, 128), 0)
    iy = lax.broadcasted_iota(jnp.int32, (ny, 128), 0)
    for k in range(q):
        hit = ix == g[k:k + 1]
        left.append(jnp.concatenate(
            [jnp.where(hit, p.astype(jnp.float32)[k:k + 1], 0.0).astype(jnp.bfloat16) for p in parts], 0))
        right.append(jnp.where(iy == y[k:k + 1], 1.0, 0.0).astype(jnp.bfloat16))
    f3 = lax.dot_general(jnp.concatenate(left, 1), jnp.concatenate(right, 1), (((1,), (1,)), ((), ())),
                         preferred_element_type=jnp.float32)
    n = tiles * nx
    fpart[...] = (f3[:n] + f3[n:2 * n] + f3[2 * n:]).reshape(tiles, nx, ny)

    pl.semaphore_wait(barrier, expected)

    copies = []
    for k in range(1, tiles):
        to = (me + k) % tiles
        c = pltpu.make_async_remote_copy(
            src_ref=fpart.at[to], dst_ref=frecv.at[k - 1], send_sem=fs_sem.at[k - 1],
            recv_sem=fr_sem.at[k - 1], device_id={"tile": to}, device_id_type=MESH)
        c.start()
        copies.append(c)
    for k in range(NZ + 2, ND):
        stack[k] = jnp.zeros((nx, ny), jnp.float32)
    for c in loads[3:]:
        c.wait()
    h0 = HALO[0]
    e0[h0:h0 + nx, :, 0:ny] = jnp.swapaxes(stack[...], 0, 1)
    for c in copies:
        c.wait()
    force = fpart[me]
    for k in range(tiles - 1):
        force = force + frecv[k]
    stack[NZ + 2] = force
    top = lax.broadcasted_iota(jnp.int32, (8, 1), 0) == 7
    for r in range(nx):
        e0[h0 + r, NZ - 8:NZ, 0:ny] += jnp.where(top, stack[NZ + 2, r:r + 1, :], 0.0)

    lane = lax.broadcasted_iota(jnp.int32, (1, 128), 1)

    def exchange(level):
        e, ps, pr, h, n, w = es[level], pss[level], prs[level], HALO[level], sizes[level], widths[level]
        wt = e.shape[2]
        npk = n // 8
        edge = ((0, 0), ((w - 1) // 128 * 128, (w - SLOT) % 128))
        for side in (0, 1):
            base, off = edge[side]
            for k in range(npk):
                acc = None
                for j in range(8):
                    v = e[h + 8 * k + j, :, base:base + 128]
                    shift = (SLOT * j - off) % 128
                    v = pltpu.roll(v, shift, 1) if shift else v
                    acc = v if acc is None else jnp.where(lane >= SLOT * j, v, acc)
                ps[side, k] = acc
        index = 0
        pending = []
        for dt in range(-REACH[level], REACH[level] + 1):
            for dc in (-1, 0, 1):
                if not (dt or dc):
                    continue
                d = abs(dt)
                if dc == 0:
                    m = min(n, h - (d - 1) * n)
                    send_lo = h if dt < 0 else h + n - m
                    land = h + d * n if dt < 0 else h - (d - 1) * n - m
                    lanes = pl.ds(0, max(w, 128))
                    src = e.at[pl.ds(send_lo, m), :, lanes]
                    dst = e.at[pl.ds(land, m), :, lanes]
                else:
                    side = 0 if dc < 0 else 1
                    slot = (-dt + REACH[level]) * 2 + (1 if dc < 0 else 0)
                    if dt == 0:
                        src, dst = ps.at[side], pr.at[slot]
                    else:
                        k = 0 if dt < 0 else npk - 1
                        src, dst = ps.at[side, pl.ds(k, 1)], pr.at[slot, pl.ds(0, 1)]
                c = pltpu.make_async_remote_copy(
                    src_ref=src, dst_ref=dst, send_sem=ss.at[level, index], recv_sem=rsem.at[level, index],
                    device_id=device(dt, dc), device_id_type=MESH)
                pending.append((c, exists(dt, dc), exists(-dt, -dc)))
                index += 1
        for c, to, _ in pending:
            pl.when(to)(c.start)
        for c, to, _ in pending:
            pl.when(to)(c.wait_send)
        for c, _, come in pending:
            pl.when(come)(c.wait_recv)
        roff = w % 128
        hb = wt - 128

        def put(row, dt, k, j):
            slot = (dt + REACH[level]) * 2
            from_left = pr[slot, k]
            from_right = pr[slot + 1, k]
            s1 = (128 - SLOT - SLOT * j) % 128
            s2 = (roff - SLOT * j) % 128
            from_left = pltpu.roll(from_left, s1, 1) if s1 else from_left
            from_right = pltpu.roll(from_right, s2, 1) if s2 else from_right
            own = e[row, :, hb:hb + 128] if roff else jnp.zeros((ND, 128), jnp.float32)
            inner = jnp.where((lane >= roff) & (lane < roff + SLOT), from_right, own)
            e[row, :, hb:hb + 128] = jnp.where(lane >= 128 - SLOT, from_left, inner)

        for r in range(n):
            put(h + r, 0, r // 8, r % 8)
        for d in range(1, REACH[level] + 1):
            m = min(n, h - (d - 1) * n)
            for r in range(m):
                put(h - (d - 1) * n - m + r, -d, 0, (n - m + r) % 8)
                put(h + d * n + r, d, 0, r % 8)

    z = lax.broadcasted_iota(jnp.int32, (1, NZ, 1), 1)

    def diag_of(k_h, k_v):
        return 4.0 * k_h + k_v * jnp.where(z > 0, 2.0, 1.0)

    def coefs(e, r, count, scale):
        return scale * e[pl.ds(r, count), NZ:NZ + 1, :], e[pl.ds(r, count), NZ + 1:NZ + 2, :]

    def over(lo, hi, step, fn, block):
        if hi - lo <= block:
            for r in range(lo, hi, step):
                fn(r)
            return

        def loop(i, carry):
            for j in range(0, block, step):
                fn(lo + i * block + j)
            return carry
        lax.fori_loop(0, (hi - lo) // block, loop, 0)
        for r in range(lo + (hi - lo) // block * block, hi, step):
            fn(r)

    def block_of(e):
        return BLOCK[[x is e for x in es].index(True)]

    def first(e, rd, u, scale, rows):
        def at(r):
            k_h, k_v = coefs(e, r, 2, scale)
            diag = 4.0 * k_h + k_v * jnp.where(z[:, 0:8] > 0, 2.0, 1.0)
            inv = jnp.where(diag > 0.0, OMEGA / diag, 0.0)
            rd[pl.ds(r, 2)] = inv
            u[pl.ds(r + 1, 2), 0:8] = inv * e[pl.ds(r, 2), 0:8, :]
            u[pl.ds(r + 1, 2), 8:16] = inv[:, 1:2] * e[pl.ds(r, 2), 8:16, :]
        over(0, rows, 2, at, block_of(e))

    def terms(e, u, r, count, scale):
        wt = u.shape[2]
        k_h, k_v = coefs(e, r, count, scale)
        x = u[pl.ds(r + 1, count)]
        hs = u[pl.ds(r, count)] + u[pl.ds(r + 2, count)]
        hs = hs + pltpu.roll(x, 1, 2) + pltpu.roll(x, wt - 1, 2)
        vs = jnp.where(z < NZ - 1, pltpu.roll(x, NZ - 1, 1), 0.0) + jnp.where(z > 0, pltpu.roll(x, 1, 1), 0.0)
        return x, e[pl.ds(r, count), 0:NZ, :] + k_h * hs + k_v * vs, k_h, k_v

    def sweep(e, rd, u, v, scale, rows, cut=0):
        def at(r):
            x, t, _, _ = terms(e, u, r, 2, scale)
            x = (1.0 - OMEGA) * x
            v[pl.ds(r + 1, 2), 0:8] = x[:, 0:8] + rd[pl.ds(r, 2)] * t[:, 0:8]
            v[pl.ds(r + 1, 2), 8:16] = x[:, 8:16] + rd[pl.ds(r, 2), 1:2] * t[:, 8:16]
        over(cut, rows - cut, 2, at, block_of(e))

    def residue(e, u, r, count, scale):
        x, t, k_h, k_v = terms(e, u, r, count, scale)
        return t - diag_of(k_h, k_v) * x

    def restrict(level, u, t):
        e, h, n, w = es[level], HALO[level], sizes[level], widths[level]
        scale = 0.25 ** level
        wt = t.shape[2]

        def at(k):
            r = h + 2 * k
            both = residue(e, u, r, 2, scale)[:, :, 0:wt]
            t[k, 0:NZ] = 0.25 * (both[0] + both[1])
            t[k, NZ:ND] = 0.25 * (e[r, NZ:ND, 0:wt] + e[r + 1, NZ:ND, 0:wt])
        over(0, n // 2, 1, at, 4)
        out = dot3(t[...].reshape(n // 2 * ND, wt), down_matrix(wt, 128))
        if w // 2 < 128:
            out = jnp.where(lane < w // 2, out, 0.0)
        es[level + 1][pl.ds(HALO[level + 1], n // 2), :, 0:128] = out.reshape(n // 2, ND, 128)

    def prolong(level, u, lo, count, fine, fine_lo):
        wt, wf = u.shape[2], fine.shape[2]
        m = up_matrix(wt, wf, widths[level - 1])
        rows = dot3(u[lo + 1:lo + 1 + count].reshape(count * NZ, wt), m).reshape(count, NZ, wf)
        for k in range(count):
            for j in range(2):
                f = fine_lo + 1 + 2 * k + j
                fine[f] = fine[f] + rows[k]

    n0, n1, n2 = (sizes[k] + 2 * HALO[k] for k in range(3))
    exchange(0)
    first(e0, rd0, ua0, 1.0, n0)
    sweep(e0, rd0, ua0, ub0, 1.0, n0, 1)
    restrict(0, ub0, t0)
    exchange(1)
    first(e1, rd1, ua1, 0.25, n1)
    sweep(e1, rd1, ua1, ub1, 0.25, n1, 1)
    restrict(1, ub1, t1)
    exchange(2)
    first(e2, rd2, ua2, 0.0625, n2)
    for k in range(3):
        sweep(e2, rd2, ua2, ub2, 0.0625, n2, 2 * k + 1)
        sweep(e2, rd2, ub2, ua2, 0.0625, n2, 2 * k + 2)
    sweep(e2, rd2, ua2, ub2, 0.0625, n2, 7)
    prolong(2, ub2, HALO[2] - 2, sizes[2] + 4, ub1, HALO[1] - 4)
    sweep(e1, rd1, ub1, ua1, 0.25, n1, 2)
    sweep(e1, rd1, ua1, ub1, 0.25, n1, 3)
    prolong(1, ub1, HALO[1] - 2, sizes[1] + 4, ub0, 0)
    sweep(e0, rd0, ub0, ua0, 1.0, n0, 2)
    sweep(e0, rd0, ua0, ub0, 1.0, n0, 3)

    def last(k):
        rfine[pl.ds(k, 2)] = residue(e0, ub0, h0 + k, 2, 1.0)[:, :, 0:ny]
    over(0, nx, 2, last, 8)
    pot[...] = jnp.swapaxes(ub0[h0 + 1:h0 + 1 + nx, :, 0:ny], 0, 1)
    res[...] = jnp.swapaxes(rfine[...], 0, 1)


def solution(mesh):
    tiles, strips, subs = mesh.shape["tile"], mesh.shape["strip"], mesh.shape["sub"]

    def body(right_side, horiz_coef, vert_coef, panel_owner, panel_cell, panel_pressure):
        nz, nx, ny = right_side.shape
        rows = [n + 2 * h for n, h in zip((nx, nx // 2, nx // 4), HALO)]
        wts = (ny + 128, ny // 2 + 128, 128)
        f32 = jnp.float32
        scratch = [
            pltpu.VMEM((tiles, nx, ny), f32),
            pltpu.VMEM((max(tiles - 1, 1), nx, ny), f32),
            pltpu.VMEM((ND, nx, ny), f32),
        ]
        scratch += [pltpu.VMEM((rows[k], ND, wts[k]), f32) for k in range(3)]
        for k in range(3):
            scratch += [pltpu.VMEM((rows[k] + 2, NZ, wts[k]), f32)] * 2 + [pltpu.VMEM((rows[k], 8, wts[k]), f32)]
        scratch += [pltpu.VMEM((nx // 2, ND, ny), f32), pltpu.VMEM((nx // 4, ND, ny // 2), f32)]
        scratch += [pltpu.VMEM((nx, NZ, ny), f32)]
        scratch += [pltpu.VMEM((2, nx // 8 >> k, ND, 128), f32) for k in range(3)]
        scratch += [pltpu.VMEM((2 * (2 * REACH[k] + 1), nx // 8 >> k, ND, 128), f32) for k in range(3)]
        panels = panel_cell.shape[0]
        scratch += [pltpu.VMEM((panels // 128, 128), t) for t in (jnp.int32, jnp.int32, f32)]
        scratch += [
            pltpu.SemaphoreType.DMA((max(tiles - 1, 1),)),
            pltpu.SemaphoreType.DMA((max(tiles - 1, 1),)),
            pltpu.SemaphoreType.DMA((3, 14)),
            pltpu.SemaphoreType.DMA((3, 14)),
            pltpu.SemaphoreType.DMA((6,)),
        ]
        out = jax.ShapeDtypeStruct((nz, nx, ny), f32)
        vmem = pl.BlockSpec(memory_space=pltpu.VMEM)
        return pl.pallas_call(
            functools.partial(kernel, (tiles, strips * subs, subs)),
            out_shape=(out, out),
            in_specs=[pl.BlockSpec(memory_space=pltpu.HBM)] * 6,
            out_specs=(vmem, vmem),
            scratch_shapes=scratch,
            compiler_params=pltpu.CompilerParams(
                collective_id=0, has_side_effects=True, vmem_limit_bytes=40 * 1024 * 1024
            ),
        )(
            right_side, horiz_coef, vert_coef,
            panel_owner.reshape(panels // 128, 128), panel_cell.reshape(panels // 128, 128),
            panel_pressure.reshape(panels // 128, 128),
        )

    return jax.shard_map(
        body,
        mesh=mesh,
        in_specs=(
            P("group", "tile", ("strip", "sub")),
            P(("group", "tile"), ("strip", "sub")),
            P(("group", "tile"), ("strip", "sub")),
            P(("group", "tile", "strip", "sub"), None),
            P(("group", "tile", "strip", "sub")),
            P(("group", "tile", "strip", "sub")),
        ),
        out_specs=(P("group", "tile", ("strip", "sub")), P("group", "tile", ("strip", "sub"))),
        check_vma=False,
    )
```

```python
import functools

import jax
import jax.numpy as jnp
from jax import lax
from jax.experimental import pallas as pl
from jax.experimental.pallas import tpu as pltpu
from jax.sharding import PartitionSpec as P

MESH = pl.DeviceIdType.MESH
OMEGA = 0.8
VMEM_BYTES = 64 * 1024 * 1024
NZ = 16
ND = 24
SLOT = 16
HALO = (4, 5, 9)
REACH = (1, 1, 2)
BLOCK = (8, 12, 26)


def split3(x):
    a = x.astype(jnp.bfloat16)
    y = x - a.astype(jnp.float32)
    b = y.astype(jnp.bfloat16)
    c = (y - b.astype(jnp.float32)).astype(jnp.bfloat16)
    return a, b, c


def dot2(x, m):
    a = x.astype(jnp.bfloat16)
    b = (x - a.astype(jnp.float32)).astype(jnp.bfloat16)
    n = x.shape[0]
    out = jnp.dot(jnp.concatenate([a, b], 0), m, preferred_element_type=jnp.float32)
    return out[:n] + out[n:]


def down_matrix(rows, cols):
    i = lax.broadcasted_iota(jnp.int32, (rows, cols), 0)
    j = lax.broadcasted_iota(jnp.int32, (rows, cols), 1)
    return jnp.where((i == 2 * j) | (i == 2 * j + 1), 1.0, 0.0).astype(jnp.bfloat16)


def up_matrix(rows, cols, local):
    i = lax.broadcasted_iota(jnp.int32, (rows, cols), 0)
    j = lax.broadcasted_iota(jnp.int32, (rows, cols), 1)
    right = (2 * i == j) | (2 * i + 1 == j)
    ib, jb = 2 * (i - rows), j - cols
    left = (ib == jb) | (ib + 1 == jb)
    hit = ((j < local + 64) & right) | ((j >= local + 64) & left)
    return jnp.where(hit, 1.0, 0.0).astype(jnp.bfloat16)


def kernel(
    dims, rs, kh, kv, owner_in, cell_in, pressure_in, pot, res,
    fpart, frecv, stack, e0, e1, e2, ua0, ub0, rd0, ua1, ub1, rd1, ua2, ub2, rd2,
    t0, t1, rfine, ps0, ps1, ps2, pr0, pr1, pr2, owner, cell, pressure, out_pot, out_res, rows_out, rows_in,
    fs_sem, fr_sem, ss, rsem, in_sem,
):
    tiles, columns, subs = dims
    nx, ny = rs.shape[1], rs.shape[2]
    sizes = (nx, nx // 2, nx // 4)
    widths = (ny, ny // 2, ny // 4)
    es, pss, prs = (e0, e1, e2), (ps0, ps1, ps2), (pr0, pr1, pr2)
    me = lax.axis_index("tile")
    col = lax.axis_index("strip") * subs + lax.axis_index("sub")

    def device(dt, dc):
        c = col + dc
        return {"tile": me + dt, "strip": c // subs, "sub": c % subs}

    def exists(dt, dc):
        ok = jnp.bool_(True)
        if dt:
            t = me + dt
            ok = ok & (t >= 0) & (t < tiles)
        if dc:
            c = col + dc
            ok = ok & (c >= 0) & (c < columns)
        return ok

    loads = [
        pltpu.make_async_copy(src, dst, in_sem.at[k])
        for k, (src, dst) in enumerate((
            (owner_in, owner), (cell_in, cell), (pressure_in, pressure),
            (rs, stack.at[pl.ds(0, NZ)]), (kh, stack.at[NZ]), (kv, stack.at[NZ + 1])))
    ]
    for c in loads:
        c.start()
    for level in range(3):
        e, h, n = es[level], HALO[level], sizes[level]
        wt = e.shape[2]
        e[0:h] = jnp.zeros((h, ND, wt), jnp.float32)
        e[h + n:] = jnp.zeros((h, ND, wt), jnp.float32)
        prs[level][...] = jnp.zeros_like(prs[level])
    rows_in[...] = jnp.zeros_like(rows_in)

    barrier = pltpu.get_barrier_semaphore()
    near = [(dt, dc) for dt in range(-2, 3) for dc in (-1, 0, 1) if dc]
    expected = jnp.int32(tiles - 1)
    for k in range(1, tiles):
        pl.semaphore_signal(barrier, inc=1, device_id={"tile": (me + k) % tiles}, device_id_type=MESH)
    for dt, dc in near:
        ok = exists(dt, dc)
        expected = expected + ok.astype(jnp.int32)

        @pl.when(ok)
        def _():
            pl.semaphore_signal(barrier, inc=1, device_id=device(dt, dc), device_id_type=MESH)

    for ref in (ua0, ub0, ua1, ub1, ua2, ub2):
        ref[0] = jnp.zeros(ref.shape[1:], jnp.float32)
        ref[ref.shape[0] - 1] = jnp.zeros(ref.shape[1:], jnp.float32)
    for c in loads[:3]:
        c.wait()

    g = owner[...] * nx + cell[...] // ny
    y = cell[...] % ny
    parts = split3(pressure[...])
    left, right = [], []
    q = g.shape[0]
    ix = lax.broadcasted_iota(jnp.int32, (tiles * nx, 128), 0)
    iy = lax.broadcasted_iota(jnp.int32, (ny, 128), 0)
    for k in range(q):
        hit = ix == g[k:k + 1]
        left.append(jnp.concatenate(
            [jnp.where(hit, p.astype(jnp.float32)[k:k + 1], 0.0).astype(jnp.bfloat16) for p in parts], 0))
        right.append(jnp.where(iy == y[k:k + 1], 1.0, 0.0).astype(jnp.bfloat16))
    f3 = lax.dot_general(jnp.concatenate(left, 1), jnp.concatenate(right, 1), (((1,), (1,)), ((), ())),
                         preferred_element_type=jnp.float32)
    n = tiles * nx
    fpart[...] = (f3[:n] + f3[n:2 * n] + f3[2 * n:]).reshape(tiles, nx, ny)

    pl.semaphore_wait(barrier, expected)

    copies = []
    for k in range(1, tiles):
        to = (me + k) % tiles
        c = pltpu.make_async_remote_copy(
            src_ref=fpart.at[to], dst_ref=frecv.at[k - 1], send_sem=fs_sem.at[k - 1],
            recv_sem=fr_sem.at[k - 1], device_id={"tile": to}, device_id_type=MESH)
        c.start()
        copies.append(c)
    for k in range(NZ + 2, ND):
        stack[k] = jnp.zeros((nx, ny), jnp.float32)
    for c in loads[3:]:
        c.wait()
    h0 = HALO[0]
    e0[h0:h0 + nx, :, 0:ny] = jnp.swapaxes(stack[...], 0, 1)
    for c in copies:
        c.wait()
    force = fpart[me]
    for k in range(tiles - 1):
        force = force + frecv[k]
    stack[NZ + 2] = force
    top = lax.broadcasted_iota(jnp.int32, (8, 1), 0) == 7
    for r in range(nx):
        e0[h0 + r, NZ - 8:NZ, 0:ny] += jnp.where(top, stack[NZ + 2, r:r + 1, :], 0.0)

    lane = lax.broadcasted_iota(jnp.int32, (1, 128), 1)

    def exchange(level):
        e, ps, pr, h, n, w = es[level], pss[level], prs[level], HALO[level], sizes[level], widths[level]
        wt = e.shape[2]
        npk = n // 8
        edge = ((0, 0), ((w - 1) // 128 * 128, (w - SLOT) % 128))
        for side in (0, 1):
            base, off = edge[side]
            for k in range(npk):
                acc = None
                for j in range(8):
                    v = e[h + 8 * k + j, :, base:base + 128]
                    shift = (SLOT * j - off) % 128
                    v = pltpu.roll(v, shift, 1) if shift else v
                    acc = v if acc is None else jnp.where(lane >= SLOT * j, v, acc)
                ps[side, k] = acc
        if level == 2:
            for k in range(n // 2):
                rows_out[k] = e[h + k] + pltpu.roll(e[h + k + n // 2], 64, 1)
        index = 0
        pending = []
        for dt in range(-REACH[level], REACH[level] + 1):
            for dc in (-1, 0, 1):
                if not (dt or dc):
                    continue
                d = abs(dt)
                if dc == 0:
                    m = min(n, h - (d - 1) * n)
                    send_lo = h if dt < 0 else h + n - m
                    land = h + d * n if dt < 0 else h - (d - 1) * n - m
                    lanes = pl.ds(0, max(w, 128))
                    src = e.at[pl.ds(send_lo, m), :, lanes]
                    dst = e.at[pl.ds(land, m), :, lanes]
                    if level == 2 and d == 1:
                        src, dst = rows_out, rows_in.at[(1 - dt) // 2]
                else:
                    side = 0 if dc < 0 else 1
                    slot = (-dt + REACH[level]) * 2 + (1 if dc < 0 else 0)
                    if dt == 0:
                        src, dst = ps.at[side], pr.at[slot]
                    else:
                        k = 0 if dt < 0 else npk - 1
                        src, dst = ps.at[side, pl.ds(k, 1)], pr.at[slot, pl.ds(0, 1)]
                c = pltpu.make_async_remote_copy(
                    src_ref=src, dst_ref=dst, send_sem=ss.at[level, index], recv_sem=rsem.at[level, index],
                    device_id=device(dt, dc), device_id_type=MESH)
                pending.append((c, exists(dt, dc), exists(-dt, -dc)))
                index += 1
        for c, to, _ in pending:
            pl.when(to)(c.start)
        for c, to, _ in pending:
            pl.when(to)(c.wait_send)
        for c, _, come in pending:
            pl.when(come)(c.wait_recv)
        if level == 2:
            for k in range(n // 2):
                for side in (0, 1):
                    row = k + h + (2 * side - 1) * n
                    both = rows_in[side, k]
                    e[row] = jnp.where(lane < w, both, 0.0)
                    e[row + n // 2] = jnp.where(lane < w, pltpu.roll(both, 64, 1), 0.0)
        roff = w % 128
        hb = wt - 128

        def put(row, dt, k, j):
            slot = (dt + REACH[level]) * 2
            from_left = pr[slot, k]
            from_right = pr[slot + 1, k]
            s1 = (128 - SLOT - SLOT * j) % 128
            s2 = (roff - SLOT * j) % 128
            from_left = pltpu.roll(from_left, s1, 1) if s1 else from_left
            from_right = pltpu.roll(from_right, s2, 1) if s2 else from_right
            own = e[row, :, hb:hb + 128] if roff else jnp.zeros((ND, 128), jnp.float32)
            inner = jnp.where((lane >= roff) & (lane < roff + SLOT), from_right, own)
            e[row, :, hb:hb + 128] = jnp.where(lane >= 128 - SLOT, from_left, inner)

        for r in range(n):
            put(h + r, 0, r // 8, r % 8)
        for d in range(1, REACH[level] + 1):
            m = min(n, h - (d - 1) * n)
            for r in range(m):
                put(h - (d - 1) * n - m + r, -d, 0, (n - m + r) % 8)
                put(h + d * n + r, d, 0, r % 8)

    z = lax.broadcasted_iota(jnp.int32, (1, NZ, 1), 1)

    def diag_of(k_h, k_v):
        return 4.0 * k_h + k_v * jnp.where(z > 0, 2.0, 1.0)

    def coefs(e, r, count, scale):
        return scale * e[pl.ds(r, count), NZ:NZ + 1, :], e[pl.ds(r, count), NZ + 1:NZ + 2, :]

    def over(lo, hi, step, fn, block):
        if hi - lo <= block:
            for r in range(lo, hi, step):
                fn(r)
            return

        def loop(i, carry):
            for j in range(0, block, step):
                fn(lo + i * block + j)
            return carry
        lax.fori_loop(0, (hi - lo) // block, loop, 0)
        for r in range(lo + (hi - lo) // block * block, hi, step):
            fn(r)

    def block_of(e):
        return BLOCK[[x is e for x in es].index(True)]

    def first(e, rd, u, scale, rows):
        def at(r):
            k_h, k_v = coefs(e, r, 2, scale)
            diag = 4.0 * k_h + k_v * jnp.where(z[:, 0:8] > 0, 2.0, 1.0)
            inv = jnp.where(diag > 0.0, OMEGA / diag, 0.0)
            rd[pl.ds(r, 2)] = inv
            u[pl.ds(r + 1, 2), 0:8] = inv * e[pl.ds(r, 2), 0:8, :]
            u[pl.ds(r + 1, 2), 8:16] = inv[:, 1:2] * e[pl.ds(r, 2), 8:16, :]
        over(0, rows, 2, at, block_of(e))

    def terms(e, u, r, count, scale):
        wt = u.shape[2]
        k_h, k_v = coefs(e, r, count, scale)
        x = u[pl.ds(r + 1, count)]
        hs = u[pl.ds(r, count)] + u[pl.ds(r + 2, count)]
        hs = hs + pltpu.roll(x, 1, 2) + pltpu.roll(x, wt - 1, 2)
        vs = jnp.where(z < NZ - 1, pltpu.roll(x, NZ - 1, 1), 0.0) + jnp.where(z > 0, pltpu.roll(x, 1, 1), 0.0)
        return x, e[pl.ds(r, count), 0:NZ, :] + k_h * hs + k_v * vs, k_h, k_v

    def sweep(e, rd, u, v, scale, rows, cut=0):
        def at(r):
            x, t, _, _ = terms(e, u, r, 2, scale)
            x = (1.0 - OMEGA) * x
            v[pl.ds(r + 1, 2), 0:8] = x[:, 0:8] + rd[pl.ds(r, 2)] * t[:, 0:8]
            v[pl.ds(r + 1, 2), 8:16] = x[:, 8:16] + rd[pl.ds(r, 2), 1:2] * t[:, 8:16]
        over(cut, rows - cut, 2, at, block_of(e))

    def residue(e, u, r, count, scale):
        x, t, k_h, k_v = terms(e, u, r, count, scale)
        return t - diag_of(k_h, k_v) * x

    def restrict(level, u, t):
        e, h, n, w = es[level], HALO[level], sizes[level], widths[level]
        scale = 0.25 ** level
        wt = t.shape[2]

        def at(k):
            r = h + 2 * k
            both = residue(e, u, r, 2, scale)[:, :, 0:wt]
            t[k, 0:NZ] = 0.25 * (both[0] + both[1])
            t[k, NZ:ND] = 0.25 * (e[r, NZ:ND, 0:wt] + e[r + 1, NZ:ND, 0:wt])
        over(0, n // 2, 1, at, 4)
        out = dot2(t[...].reshape(n // 2 * ND, wt), down_matrix(wt, 128))
        if w // 2 < 128:
            out = jnp.where(lane < w // 2, out, 0.0)
        es[level + 1][pl.ds(HALO[level + 1], n // 2), :, 0:128] = out.reshape(n // 2, ND, 128)

    def prolong(level, u, lo, count, fine, fine_lo):
        wt, wf = u.shape[2], fine.shape[2]
        m = up_matrix(wt, wf, widths[level - 1])
        rows = dot2(u[lo + 1:lo + 1 + count].reshape(count * NZ, wt), m).reshape(count, NZ, wf)
        for k in range(count):
            for j in range(2):
                f = fine_lo + 1 + 2 * k + j
                fine[f] = fine[f] + rows[k]

    n0, n1, n2 = (sizes[k] + 2 * HALO[k] for k in range(3))
    exchange(0)
    first(e0, rd0, ua0, 1.0, n0)
    sweep(e0, rd0, ua0, ub0, 1.0, n0, 1)
    restrict(0, ub0, t0)
    exchange(1)
    first(e1, rd1, ua1, 0.25, n1)
    sweep(e1, rd1, ua1, ub1, 0.25, n1, 1)
    restrict(1, ub1, t1)
    exchange(2)
    first(e2, rd2, ua2, 0.0625, n2)
    for k in range(3):
        sweep(e2, rd2, ua2, ub2, 0.0625, n2, 2 * k + 1)
        sweep(e2, rd2, ub2, ua2, 0.0625, n2, 2 * k + 2)
    sweep(e2, rd2, ua2, ub2, 0.0625, n2, 7)
    prolong(2, ub2, HALO[2] - 2, sizes[2] + 4, ub1, HALO[1] - 4)
    sweep(e1, rd1, ub1, ua1, 0.25, n1, 2)
    sweep(e1, rd1, ua1, ub1, 0.25, n1, 3)
    prolong(1, ub1, HALO[1] - 2, sizes[1] + 4, ub0, 0)
    sweep(e0, rd0, ub0, ua0, 1.0, n0, 2)
    sweep(e0, rd0, ua0, ub0, 1.0, n0, 3)

    out_pot[...] = jnp.swapaxes(ub0[h0 + 1:h0 + 1 + nx, :, 0:ny], 0, 1)
    store = pltpu.make_async_copy(out_pot, pot, in_sem.at[6])
    store.start()

    def last(k):
        rfine[pl.ds(k, 2)] = residue(e0, ub0, h0 + k, 2, 1.0)[:, :, 0:ny]
    over(0, nx, 2, last, 8)
    out_res[...] = jnp.swapaxes(rfine[...], 0, 1)
    final = pltpu.make_async_copy(out_res, res, in_sem.at[7])
    final.start()
    store.wait()
    final.wait()


def solution(mesh):
    tiles, strips, subs = mesh.shape["tile"], mesh.shape["strip"], mesh.shape["sub"]

    def body(right_side, horiz_coef, vert_coef, panel_owner, panel_cell, panel_pressure):
        nz, nx, ny = right_side.shape
        rows = [n + 2 * h for n, h in zip((nx, nx // 2, nx // 4), HALO)]
        wts = (ny + 128, ny // 2 + 128, 128)
        f32 = jnp.float32
        scratch = [
            pltpu.VMEM((tiles, nx, ny), f32),
            pltpu.VMEM((max(tiles - 1, 1), nx, ny), f32),
            pltpu.VMEM((ND, nx, ny), f32),
        ]
        scratch += [pltpu.VMEM((rows[k], ND, wts[k]), f32) for k in range(3)]
        for k in range(3):
            scratch += [pltpu.VMEM((rows[k] + 2, NZ, wts[k]), f32)] * 2 + [pltpu.VMEM((rows[k], 8, wts[k]), f32)]
        scratch += [pltpu.VMEM((nx // 2, ND, ny), f32), pltpu.VMEM((nx // 4, ND, ny // 2), f32)]
        scratch += [pltpu.VMEM((nx, NZ, ny), f32)]
        scratch += [pltpu.VMEM((2, nx // 8 >> k, ND, 128), f32) for k in range(3)]
        scratch += [pltpu.VMEM((2 * (2 * REACH[k] + 1), nx // 8 >> k, ND, 128), f32) for k in range(3)]
        panels = panel_cell.shape[0]
        scratch += [pltpu.VMEM((panels // 128, 128), t) for t in (jnp.int32, jnp.int32, f32)]
        scratch += [pltpu.VMEM((nz, nx, ny), f32)] * 2
        half = nx // 8
        scratch += [pltpu.VMEM((half, ND, 128), f32), pltpu.VMEM((2, half, ND, 128), f32)]
        scratch += [
            pltpu.SemaphoreType.DMA((max(tiles - 1, 1),)),
            pltpu.SemaphoreType.DMA((max(tiles - 1, 1),)),
            pltpu.SemaphoreType.DMA((3, 14)),
            pltpu.SemaphoreType.DMA((3, 14)),
            pltpu.SemaphoreType.DMA((8,)),
        ]
        out = jax.ShapeDtypeStruct((nz, nx, ny), f32)
        hbm = pl.BlockSpec(memory_space=pltpu.HBM)
        return pl.pallas_call(
            functools.partial(kernel, (tiles, strips * subs, subs)),
            out_shape=(out, out),
            in_specs=[hbm] * 6,
            out_specs=(hbm, hbm),
            scratch_shapes=scratch,
            compiler_params=pltpu.CompilerParams(
                collective_id=0, has_side_effects=True, vmem_limit_bytes=VMEM_BYTES
            ),
        )(
            right_side, horiz_coef, vert_coef,
            panel_owner.reshape(panels // 128, 128), panel_cell.reshape(panels // 128, 128),
            panel_pressure.reshape(panels // 128, 128),
        )

    return jax.shard_map(
        body,
        mesh=mesh,
        in_specs=(
            P("group", "tile", ("strip", "sub")),
            P(("group", "tile"), ("strip", "sub")),
            P(("group", "tile"), ("strip", "sub")),
            P(("group", "tile", "strip", "sub"), None),
            P(("group", "tile", "strip", "sub")),
            P(("group", "tile", "strip", "sub")),
        ),
        out_specs=(P("group", "tile", ("strip", "sub")), P("group", "tile", ("strip", "sub"))),
        check_vma=False,
    )
```

```python
import functools

import jax
import jax.numpy as jnp
from jax import lax
from jax.experimental import pallas as pl
from jax.experimental.pallas import tpu as pltpu
from jax.sharding import PartitionSpec as P

MESH = pl.DeviceIdType.MESH
OMEGA = 0.8
VMEM_BYTES = 64 * 1024 * 1024
NZ = 16
ND = 24
SLOT = 16
HALO = (4, 5, 9)
REACH = (1, 1, 2)
BLOCK = (8, 12, 26)


def split3(x):
    a = x.astype(jnp.bfloat16)
    y = x - a.astype(jnp.float32)
    b = y.astype(jnp.bfloat16)
    c = (y - b.astype(jnp.float32)).astype(jnp.bfloat16)
    return a, b, c


def dot2(x, m):
    a = x.astype(jnp.bfloat16)
    b = (x - a.astype(jnp.float32)).astype(jnp.bfloat16)
    n = x.shape[0]
    out = jnp.dot(jnp.concatenate([a, b], 0), m, preferred_element_type=jnp.float32)
    return out[:n] + out[n:]


def down_matrix(rows, cols):
    i = lax.broadcasted_iota(jnp.int32, (rows, cols), 0)
    j = lax.broadcasted_iota(jnp.int32, (rows, cols), 1)
    return jnp.where((i == 2 * j) | (i == 2 * j + 1), 1.0, 0.0).astype(jnp.bfloat16)


def up_matrix(rows, cols, local):
    i = lax.broadcasted_iota(jnp.int32, (rows, cols), 0)
    j = lax.broadcasted_iota(jnp.int32, (rows, cols), 1)
    right = (2 * i == j) | (2 * i + 1 == j)
    ib, jb = 2 * (i - rows), j - cols
    left = (ib == jb) | (ib + 1 == jb)
    hit = ((j < local + 64) & right) | ((j >= local + 64) & left)
    return jnp.where(hit, 1.0, 0.0).astype(jnp.bfloat16)


def kernel(
    dims, rs, kh, kv, owner_in, cell_in, pressure_in, pot, res,
    fpart, frecv, stack, e0, e1, e2, ua0, ub0, rd0, ua1, ub1, rd1, ua2, ub2, rd2,
    t0, t1, rfine, ps0, ps1, ps2, pr0, pr1, pr2, owner, cell, pressure, out_pot, out_res, rows_out, rows_in,
    fs_sem, fr_sem, ss, rsem, in_sem,
):
    tiles, columns, subs = dims
    nx, ny = rs.shape[1], rs.shape[2]
    sizes = (nx, nx // 2, nx // 4)
    widths = (ny, ny // 2, ny // 4)
    es, pss, prs = (e0, e1, e2), (ps0, ps1, ps2), (pr0, pr1, pr2)
    me = lax.axis_index("tile")
    col = lax.axis_index("strip") * subs + lax.axis_index("sub")

    def device(dt, dc):
        c = col + dc
        return {"tile": me + dt, "strip": c // subs, "sub": c % subs}

    def exists(dt, dc):
        ok = jnp.bool_(True)
        if dt:
            t = me + dt
            ok = ok & (t >= 0) & (t < tiles)
        if dc:
            c = col + dc
            ok = ok & (c >= 0) & (c < columns)
        return ok

    loads = [
        pltpu.make_async_copy(src, dst, in_sem.at[k])
        for k, (src, dst) in enumerate((
            (owner_in, owner), (cell_in, cell), (pressure_in, pressure),
            (rs, stack.at[pl.ds(0, NZ)]), (kh, stack.at[NZ]), (kv, stack.at[NZ + 1])))
    ]
    for c in loads:
        c.start()
    for level in range(3):
        e, h, n = es[level], HALO[level], sizes[level]
        wt = e.shape[2]
        e[0:h] = jnp.zeros((h, ND, wt), jnp.float32)
        e[h + n:] = jnp.zeros((h, ND, wt), jnp.float32)
        prs[level][...] = jnp.zeros_like(prs[level])
    rows_in[...] = jnp.zeros_like(rows_in)

    barrier = pltpu.get_barrier_semaphore()
    near = [(dt, dc) for dt in range(-2, 3) for dc in (-1, 0, 1) if dc]
    expected = jnp.int32(tiles - 1)
    for k in range(1, tiles):
        pl.semaphore_signal(barrier, inc=1, device_id={"tile": (me + k) % tiles}, device_id_type=MESH)
    for dt, dc in near:
        ok = exists(dt, dc)
        expected = expected + ok.astype(jnp.int32)

        @pl.when(ok)
        def _():
            pl.semaphore_signal(barrier, inc=1, device_id=device(dt, dc), device_id_type=MESH)

    for ref in (ua0, ub0, ua1, ub1, ua2, ub2):
        ref[0] = jnp.zeros(ref.shape[1:], jnp.float32)
        ref[ref.shape[0] - 1] = jnp.zeros(ref.shape[1:], jnp.float32)
    for c in loads[:3]:
        c.wait()

    g = owner[...] * nx + cell[...] // ny
    y = cell[...] % ny
    parts = split3(pressure[...])
    left, right = [], []
    q = g.shape[0]
    ix = lax.broadcasted_iota(jnp.int32, (tiles * nx, 128), 0)
    iy = lax.broadcasted_iota(jnp.int32, (ny, 128), 0)
    for k in range(q):
        hit = ix == g[k:k + 1]
        left.append(jnp.concatenate(
            [jnp.where(hit, p.astype(jnp.float32)[k:k + 1], 0.0).astype(jnp.bfloat16) for p in parts], 0))
        right.append(jnp.where(iy == y[k:k + 1], 1.0, 0.0).astype(jnp.bfloat16))
    f3 = lax.dot_general(jnp.concatenate(left, 1), jnp.concatenate(right, 1), (((1,), (1,)), ((), ())),
                         preferred_element_type=jnp.float32)
    n = tiles * nx
    fpart[...] = (f3[:n] + f3[n:2 * n] + f3[2 * n:]).reshape(tiles, nx, ny)

    pl.semaphore_wait(barrier, expected)

    copies = []
    for k in range(1, tiles):
        to = (me + k) % tiles
        c = pltpu.make_async_remote_copy(
            src_ref=fpart.at[to], dst_ref=frecv.at[k - 1], send_sem=fs_sem.at[k - 1],
            recv_sem=fr_sem.at[k - 1], device_id={"tile": to}, device_id_type=MESH)
        c.start()
        copies.append(c)
    for k in range(NZ + 2, ND):
        stack[k] = jnp.zeros((nx, ny), jnp.float32)
    for c in loads[3:]:
        c.wait()
    h0 = HALO[0]
    e0[h0:h0 + nx, :, 0:ny] = jnp.swapaxes(stack[...], 0, 1)
    for c in copies:
        c.wait()
    force = fpart[me]
    for k in range(tiles - 1):
        force = force + frecv[k]
    stack[NZ + 2] = force
    top = lax.broadcasted_iota(jnp.int32, (8, 1), 0) == 7
    for r in range(nx):
        e0[h0 + r, NZ - 8:NZ, 0:ny] += jnp.where(top, stack[NZ + 2, r:r + 1, :], 0.0)

    lane = lax.broadcasted_iota(jnp.int32, (1, 128), 1)

    def exchange(level, meanwhile=None):
        e, ps, pr, h, n, w = es[level], pss[level], prs[level], HALO[level], sizes[level], widths[level]
        wt = e.shape[2]
        npk = n // 8
        edge = ((0, 0), ((w - 1) // 128 * 128, (w - SLOT) % 128))
        for side in (0, 1):
            base, off = edge[side]
            for k in range(npk):
                acc = None
                for j in range(8):
                    v = e[h + 8 * k + j, :, base:base + 128]
                    shift = (SLOT * j - off) % 128
                    v = pltpu.roll(v, shift, 1) if shift else v
                    acc = v if acc is None else jnp.where(lane >= SLOT * j, v, acc)
                ps[side, k] = acc
        if level == 2:
            for k in range(n // 2):
                rows_out[k] = e[h + k] + pltpu.roll(e[h + k + n // 2], 64, 1)
        index = 0
        pending = []
        for dt in range(-REACH[level], REACH[level] + 1):
            for dc in (-1, 0, 1):
                if not (dt or dc):
                    continue
                d = abs(dt)
                if dc == 0:
                    m = min(n, h - (d - 1) * n)
                    send_lo = h if dt < 0 else h + n - m
                    land = h + d * n if dt < 0 else h - (d - 1) * n - m
                    lanes = pl.ds(0, max(w, 128))
                    src = e.at[pl.ds(send_lo, m), :, lanes]
                    dst = e.at[pl.ds(land, m), :, lanes]
                    if level == 2 and d == 1:
                        src, dst = rows_out, rows_in.at[(1 - dt) // 2]
                else:
                    side = 0 if dc < 0 else 1
                    slot = (-dt + REACH[level]) * 2 + (1 if dc < 0 else 0)
                    if dt == 0:
                        src, dst = ps.at[side], pr.at[slot]
                    else:
                        k = 0 if dt < 0 else npk - 1
                        src, dst = ps.at[side, pl.ds(k, 1)], pr.at[slot, pl.ds(0, 1)]
                c = pltpu.make_async_remote_copy(
                    src_ref=src, dst_ref=dst, send_sem=ss.at[level, index], recv_sem=rsem.at[level, index],
                    device_id=device(dt, dc), device_id_type=MESH)
                pending.append((c, exists(dt, dc), exists(-dt, -dc)))
                index += 1
        for c, to, _ in pending:
            pl.when(to)(c.start)
        if meanwhile is not None:
            meanwhile()
        for c, to, _ in pending:
            pl.when(to)(c.wait_send)
        for c, _, come in pending:
            pl.when(come)(c.wait_recv)
        if level == 2:
            for k in range(n // 2):
                for side in (0, 1):
                    row = k + h + (2 * side - 1) * n
                    both = rows_in[side, k]
                    e[row] = jnp.where(lane < w, both, 0.0)
                    e[row + n // 2] = jnp.where(lane < w, pltpu.roll(both, 64, 1), 0.0)
        roff = w % 128
        hb = wt - 128

        def put(row, dt, k, j):
            slot = (dt + REACH[level]) * 2
            from_left = pr[slot, k]
            from_right = pr[slot + 1, k]
            s1 = (128 - SLOT - SLOT * j) % 128
            s2 = (roff - SLOT * j) % 128
            from_left = pltpu.roll(from_left, s1, 1) if s1 else from_left
            from_right = pltpu.roll(from_right, s2, 1) if s2 else from_right
            own = e[row, :, hb:hb + 128] if roff else jnp.zeros((ND, 128), jnp.float32)
            inner = jnp.where((lane >= roff) & (lane < roff + SLOT), from_right, own)
            e[row, :, hb:hb + 128] = jnp.where(lane >= 128 - SLOT, from_left, inner)

        for r in range(n):
            put(h + r, 0, r // 8, r % 8)
        for d in range(1, REACH[level] + 1):
            m = min(n, h - (d - 1) * n)
            for r in range(m):
                put(h - (d - 1) * n - m + r, -d, 0, (n - m + r) % 8)
                put(h + d * n + r, d, 0, r % 8)

    z = lax.broadcasted_iota(jnp.int32, (1, NZ, 1), 1)

    def diag_of(k_h, k_v):
        return 4.0 * k_h + k_v * jnp.where(z > 0, 2.0, 1.0)

    def coefs(e, r, count, scale):
        return scale * e[pl.ds(r, count), NZ:NZ + 1, :], e[pl.ds(r, count), NZ + 1:NZ + 2, :]

    def over(lo, hi, step, fn, block):
        if hi - lo <= block:
            for r in range(lo, hi, step):
                fn(r)
            return

        def loop(i, carry):
            for j in range(0, block, step):
                fn(lo + i * block + j)
            return carry
        lax.fori_loop(0, (hi - lo) // block, loop, 0)
        for r in range(lo + (hi - lo) // block * block, hi, step):
            fn(r)

    def block_of(e):
        return BLOCK[[x is e for x in es].index(True)]

    def first(e, rd, u, scale, lo, hi, lanes):
        def at(r, count=2):
            here, up = pl.ds(r, count), pl.ds(r + 1, count)
            k_h = scale * e[here, NZ:NZ + 1, lanes]
            k_v = e[here, NZ + 1:NZ + 2, lanes]
            diag = 4.0 * k_h + k_v * jnp.where(z[:, 0:8] > 0, 2.0, 1.0)
            inv = jnp.where(diag > 0.0, OMEGA / diag, 0.0)
            rd[here, :, lanes] = inv
            u[up, 0:8, lanes] = inv * e[here, 0:8, lanes]
            u[up, 8:16, lanes] = inv[:, 1:2] * e[here, 8:16, lanes]
        even = hi - (hi - lo) % 2
        over(lo, even, 2, at, block_of(e))
        if even < hi:
            at(even, 1)

    def terms(e, u, r, count, scale):
        wt = u.shape[2]
        k_h, k_v = coefs(e, r, count, scale)
        x = u[pl.ds(r + 1, count)]
        hs = u[pl.ds(r, count)] + u[pl.ds(r + 2, count)]
        hs = hs + pltpu.roll(x, 1, 2) + pltpu.roll(x, wt - 1, 2)
        vs = jnp.where(z < NZ - 1, pltpu.roll(x, NZ - 1, 1), 0.0) + jnp.where(z > 0, pltpu.roll(x, 1, 1), 0.0)
        return x, e[pl.ds(r, count), 0:NZ, :] + k_h * hs + k_v * vs, k_h, k_v

    def sweep(e, rd, u, v, scale, rows, cut=0):
        def at(r):
            x, t, _, _ = terms(e, u, r, 2, scale)
            x = (1.0 - OMEGA) * x
            v[pl.ds(r + 1, 2), 0:8] = x[:, 0:8] + rd[pl.ds(r, 2)] * t[:, 0:8]
            v[pl.ds(r + 1, 2), 8:16] = x[:, 8:16] + rd[pl.ds(r, 2), 1:2] * t[:, 8:16]
        over(cut, rows - cut, 2, at, block_of(e))

    def residue(e, u, r, count, scale):
        x, t, k_h, k_v = terms(e, u, r, count, scale)
        return t - diag_of(k_h, k_v) * x

    def restrict(level, u, t):
        e, h, n, w = es[level], HALO[level], sizes[level], widths[level]
        scale = 0.25 ** level
        wt = t.shape[2]

        def at(k):
            r = h + 2 * k
            both = residue(e, u, r, 2, scale)[:, :, 0:wt]
            t[k, 0:NZ] = 0.25 * (both[0] + both[1])
            t[k, NZ:ND] = 0.25 * (e[r, NZ:ND, 0:wt] + e[r + 1, NZ:ND, 0:wt])
        over(0, n // 2, 1, at, 4)
        out = dot2(t[...].reshape(n // 2 * ND, wt), down_matrix(wt, 128))
        if w // 2 < 128:
            out = jnp.where(lane < w // 2, out, 0.0)
        es[level + 1][pl.ds(HALO[level + 1], n // 2), :, 0:128] = out.reshape(n // 2, ND, 128)

    def prolong(level, u, lo, count, fine, fine_lo):
        wt, wf = u.shape[2], fine.shape[2]
        m = up_matrix(wt, wf, widths[level - 1])
        rows = dot2(u[lo + 1:lo + 1 + count].reshape(count * NZ, wt), m).reshape(count, NZ, wf)
        for k in range(count):
            for j in range(2):
                f = fine_lo + 1 + 2 * k + j
                fine[f] = fine[f] + rows[k]

    n0, n1, n2 = (sizes[k] + 2 * HALO[k] for k in range(3))
    def own(level, e, rd, u):
        h, n, w = HALO[level], sizes[level], widths[level]
        first(e, rd, u, 0.25 ** level, h, h + n, slice(0, w))

    def rest(level, e, rd, u):
        h, n, w, wt = HALO[level], sizes[level], widths[level], e.shape[2]
        first(e, rd, u, 0.25 ** level, 0, h, slice(0, wt))
        first(e, rd, u, 0.25 ** level, h, h + n, slice(w, wt))
        first(e, rd, u, 0.25 ** level, h + n, 2 * h + n, slice(0, wt))

    exchange(0, lambda: own(0, e0, rd0, ua0))
    rest(0, e0, rd0, ua0)
    sweep(e0, rd0, ua0, ub0, 1.0, n0, 1)
    restrict(0, ub0, t0)
    exchange(1, lambda: own(1, e1, rd1, ua1))
    rest(1, e1, rd1, ua1)
    sweep(e1, rd1, ua1, ub1, 0.25, n1, 1)
    restrict(1, ub1, t1)
    exchange(2)
    first(e2, rd2, ua2, 0.0625, 0, n2, slice(0, 128))
    for k in range(3):
        sweep(e2, rd2, ua2, ub2, 0.0625, n2, 2 * k + 1)
        sweep(e2, rd2, ub2, ua2, 0.0625, n2, 2 * k + 2)
    sweep(e2, rd2, ua2, ub2, 0.0625, n2, 7)
    prolong(2, ub2, HALO[2] - 2, sizes[2] + 4, ub1, HALO[1] - 4)
    sweep(e1, rd1, ub1, ua1, 0.25, n1, 2)
    sweep(e1, rd1, ua1, ub1, 0.25, n1, 3)
    prolong(1, ub1, HALO[1] - 2, sizes[1] + 4, ub0, 0)
    sweep(e0, rd0, ub0, ua0, 1.0, n0, 2)
    sweep(e0, rd0, ua0, ub0, 1.0, n0, 3)

    out_pot[...] = jnp.swapaxes(ub0[h0 + 1:h0 + 1 + nx, :, 0:ny], 0, 1)
    store = pltpu.make_async_copy(out_pot, pot, in_sem.at[6])
    store.start()

    def last(k):
        rfine[pl.ds(k, 2)] = residue(e0, ub0, h0 + k, 2, 1.0)[:, :, 0:ny]
    over(0, nx, 2, last, 8)
    out_res[...] = jnp.swapaxes(rfine[...], 0, 1)
    final = pltpu.make_async_copy(out_res, res, in_sem.at[7])
    final.start()
    store.wait()
    final.wait()


def hand_over(a, b, c, d, sems):
    part = a.shape[0] // 4
    copies = []
    for k in range(4):
        for j, (src, dst) in enumerate(((a, c), (b, d))):
            rows = pl.ds(k * part, part)
            copies.append(pltpu.make_async_copy(src.at[rows], dst.at[rows], sems.at[2 * k + j]))
            copies[-1].start()
    for c in copies:
        c.wait()


def solution(mesh):
    tiles, strips, subs = mesh.shape["tile"], mesh.shape["strip"], mesh.shape["sub"]

    def body(right_side, horiz_coef, vert_coef, panel_owner, panel_cell, panel_pressure):
        nz, nx, ny = right_side.shape
        rows = [n + 2 * h for n, h in zip((nx, nx // 2, nx // 4), HALO)]
        wts = (ny + 128, ny // 2 + 128, 128)
        f32 = jnp.float32
        scratch = [
            pltpu.VMEM((tiles, nx, ny), f32),
            pltpu.VMEM((max(tiles - 1, 1), nx, ny), f32),
            pltpu.VMEM((ND, nx, ny), f32),
        ]
        scratch += [pltpu.VMEM((rows[k], ND, wts[k]), f32) for k in range(3)]
        for k in range(3):
            scratch += [pltpu.VMEM((rows[k] + 2, NZ, wts[k]), f32)] * 2 + [pltpu.VMEM((rows[k], 8, wts[k]), f32)]
        scratch += [pltpu.VMEM((nx // 2, ND, ny), f32), pltpu.VMEM((nx // 4, ND, ny // 2), f32)]
        scratch += [pltpu.VMEM((nx, NZ, ny), f32)]
        scratch += [pltpu.VMEM((2, nx // 8 >> k, ND, 128), f32) for k in range(3)]
        scratch += [pltpu.VMEM((2 * (2 * REACH[k] + 1), nx // 8 >> k, ND, 128), f32) for k in range(3)]
        panels = panel_cell.shape[0]
        scratch += [pltpu.VMEM((panels // 128, 128), t) for t in (jnp.int32, jnp.int32, f32)]
        scratch += [pltpu.VMEM((nz, nx, ny), f32)] * 2
        half = nx // 8
        scratch += [pltpu.VMEM((half, ND, 128), f32), pltpu.VMEM((2, half, ND, 128), f32)]
        scratch += [
            pltpu.SemaphoreType.DMA((max(tiles - 1, 1),)),
            pltpu.SemaphoreType.DMA((max(tiles - 1, 1),)),
            pltpu.SemaphoreType.DMA((3, 14)),
            pltpu.SemaphoreType.DMA((3, 14)),
            pltpu.SemaphoreType.DMA((8,)),
        ]
        out = jax.ShapeDtypeStruct((nz, nx, ny), f32)
        hbm = pl.BlockSpec(memory_space=pltpu.HBM)
        made = pl.pallas_call(
            functools.partial(kernel, (tiles, strips * subs, subs)),
            out_shape=(out, out),
            in_specs=[hbm] * 6,
            out_specs=(hbm, hbm),
            scratch_shapes=scratch,
            compiler_params=pltpu.CompilerParams(
                collective_id=0, has_side_effects=True, vmem_limit_bytes=VMEM_BYTES
            ),
        )(
            right_side, horiz_coef, vert_coef,
            panel_owner.reshape(panels // 128, 128), panel_cell.reshape(panels // 128, 128),
            panel_pressure.reshape(panels // 128, 128),
        )
        return pl.pallas_call(
            hand_over,
            out_shape=(out, out),
            in_specs=[hbm] * 2,
            out_specs=(hbm, hbm),
            scratch_shapes=[pltpu.SemaphoreType.DMA((8,))],
            compiler_params=pltpu.CompilerParams(vmem_limit_bytes=VMEM_BYTES),
        )(*made)

    return jax.shard_map(
        body,
        mesh=mesh,
        in_specs=(
            P("group", "tile", ("strip", "sub")),
            P(("group", "tile"), ("strip", "sub")),
            P(("group", "tile"), ("strip", "sub")),
            P(("group", "tile", "strip", "sub"), None),
            P(("group", "tile", "strip", "sub")),
            P(("group", "tile", "strip", "sub")),
        ),
        out_specs=(P("group", "tile", ("strip", "sub")), P("group", "tile", ("strip", "sub"))),
        check_vma=False,
    )
```

```python
import functools

import jax
import jax.numpy as jnp
from jax import lax
from jax.experimental import pallas as pl
from jax.experimental.pallas import tpu as pltpu
from jax.sharding import PartitionSpec as P

MESH = pl.DeviceIdType.MESH
OMEGA = 0.8
VMEM_BYTES = 64 * 1024 * 1024
NZ = 16
ND = 24
SLOT = 16
HALO = (4, 5, 9)
REACH = (1, 1, 2)
BLOCK = (8, 12, 26)


def split3(x):
    a = x.astype(jnp.bfloat16)
    y = x - a.astype(jnp.float32)
    b = y.astype(jnp.bfloat16)
    c = (y - b.astype(jnp.float32)).astype(jnp.bfloat16)
    return a, b, c


def dot2(x, m):
    a = x.astype(jnp.bfloat16)
    b = (x - a.astype(jnp.float32)).astype(jnp.bfloat16)
    n = x.shape[0]
    out = jnp.dot(jnp.concatenate([a, b], 0), m, preferred_element_type=jnp.float32)
    return out[:n] + out[n:]


def down_matrix(rows, cols):
    i = lax.broadcasted_iota(jnp.int32, (rows, cols), 0)
    j = lax.broadcasted_iota(jnp.int32, (rows, cols), 1)
    return jnp.where((i == 2 * j) | (i == 2 * j + 1), 1.0, 0.0).astype(jnp.bfloat16)


def up_matrix(rows, cols, local):
    i = lax.broadcasted_iota(jnp.int32, (rows, cols), 0)
    j = lax.broadcasted_iota(jnp.int32, (rows, cols), 1)
    right = (2 * i == j) | (2 * i + 1 == j)
    ib, jb = 2 * (i - rows), j - cols
    left = (ib == jb) | (ib + 1 == jb)
    hit = ((j < local + 64) & right) | ((j >= local + 64) & left)
    return jnp.where(hit, 1.0, 0.0).astype(jnp.bfloat16)


def kernel(
    dims, rs, kh, kv, owner_in, cell_in, pressure_in, pot, res,
    fpart, frecv, stack, e0, e1, e2, ua0, ub0, rd0, ua1, ub1, rd1, ua2, ub2, rd2,
    t0, t1, rfine, ps0, ps1, ps2, pr0, pr1, pr2, owner, cell, pressure, rows_out, rows_in,
    fs_sem, fr_sem, ss, rsem, in_sem,
):
    tiles, columns, subs = dims
    nx, ny = rs.shape[1], rs.shape[2]
    sizes = (nx, nx // 2, nx // 4)
    widths = (ny, ny // 2, ny // 4)
    es, pss, prs = (e0, e1, e2), (ps0, ps1, ps2), (pr0, pr1, pr2)
    me = lax.axis_index("tile")
    col = lax.axis_index("strip") * subs + lax.axis_index("sub")

    def device(dt, dc):
        c = col + dc
        return {"tile": me + dt, "strip": c // subs, "sub": c % subs}

    def exists(dt, dc):
        ok = jnp.bool_(True)
        if dt:
            t = me + dt
            ok = ok & (t >= 0) & (t < tiles)
        if dc:
            c = col + dc
            ok = ok & (c >= 0) & (c < columns)
        return ok

    loads = [
        pltpu.make_async_copy(src, dst, in_sem.at[k])
        for k, (src, dst) in enumerate((
            (owner_in, owner), (cell_in, cell), (pressure_in, pressure),
            (rs, stack.at[pl.ds(0, NZ)]), (kh, stack.at[NZ]), (kv, stack.at[NZ + 1])))
    ]
    for c in loads:
        c.start()
    for level in range(3):
        e, h, n = es[level], HALO[level], sizes[level]
        wt = e.shape[2]
        e[0:h] = jnp.zeros((h, ND, wt), jnp.float32)
        e[h + n:] = jnp.zeros((h, ND, wt), jnp.float32)
        prs[level][...] = jnp.zeros_like(prs[level])
    rows_in[...] = jnp.zeros_like(rows_in)

    barrier = pltpu.get_barrier_semaphore()
    near = [(dt, dc) for dt in range(-2, 3) for dc in (-1, 0, 1) if dc]
    expected = jnp.int32(tiles - 1)
    for k in range(1, tiles):
        pl.semaphore_signal(barrier, inc=1, device_id={"tile": (me + k) % tiles}, device_id_type=MESH)
    for dt, dc in near:
        ok = exists(dt, dc)
        expected = expected + ok.astype(jnp.int32)

        @pl.when(ok)
        def _():
            pl.semaphore_signal(barrier, inc=1, device_id=device(dt, dc), device_id_type=MESH)

    for ref in (ua0, ub0, ua1, ub1, ua2, ub2):
        ref[0] = jnp.zeros(ref.shape[1:], jnp.float32)
        ref[ref.shape[0] - 1] = jnp.zeros(ref.shape[1:], jnp.float32)
    for c in loads[:3]:
        c.wait()

    g = owner[...] * nx + cell[...] // ny
    y = cell[...] % ny
    parts = split3(pressure[...])
    left, right = [], []
    q = g.shape[0]
    ix = lax.broadcasted_iota(jnp.int32, (tiles * nx, 128), 0)
    iy = lax.broadcasted_iota(jnp.int32, (ny, 128), 0)
    for k in range(q):
        hit = ix == g[k:k + 1]
        left.append(jnp.concatenate(
            [jnp.where(hit, p.astype(jnp.float32)[k:k + 1], 0.0).astype(jnp.bfloat16) for p in parts], 0))
        right.append(jnp.where(iy == y[k:k + 1], 1.0, 0.0).astype(jnp.bfloat16))
    f3 = lax.dot_general(jnp.concatenate(left, 1), jnp.concatenate(right, 1), (((1,), (1,)), ((), ())),
                         preferred_element_type=jnp.float32)
    n = tiles * nx
    fpart[...] = (f3[:n] + f3[n:2 * n] + f3[2 * n:]).reshape(tiles, nx, ny)

    pl.semaphore_wait(barrier, expected)

    copies = []
    for k in range(1, tiles):
        to = (me + k) % tiles
        c = pltpu.make_async_remote_copy(
            src_ref=fpart.at[to], dst_ref=frecv.at[k - 1], send_sem=fs_sem.at[k - 1],
            recv_sem=fr_sem.at[k - 1], device_id={"tile": to}, device_id_type=MESH)
        c.start()
        copies.append(c)
    for k in range(NZ + 2, ND):
        stack[k] = jnp.zeros((nx, ny), jnp.float32)
    for c in loads[3:]:
        c.wait()
    h0 = HALO[0]
    e0[h0:h0 + nx, :, 0:ny] = jnp.swapaxes(stack[...], 0, 1)
    for c in copies:
        c.wait()
    force = fpart[me]
    for k in range(tiles - 1):
        force = force + frecv[k]
    stack[NZ + 2] = force
    top = lax.broadcasted_iota(jnp.int32, (8, 1), 0) == 7
    for r in range(nx):
        e0[h0 + r, NZ - 8:NZ, 0:ny] += jnp.where(top, stack[NZ + 2, r:r + 1, :], 0.0)

    lane = lax.broadcasted_iota(jnp.int32, (1, 128), 1)

    def exchange(level, meanwhile=None):
        e, ps, pr, h, n, w = es[level], pss[level], prs[level], HALO[level], sizes[level], widths[level]
        wt = e.shape[2]
        npk = n // 8
        edge = ((0, 0), ((w - 1) // 128 * 128, (w - SLOT) % 128))
        for side in (0, 1):
            base, off = edge[side]
            for k in range(npk):
                acc = None
                for j in range(8):
                    v = e[h + 8 * k + j, :, base:base + 128]
                    shift = (SLOT * j - off) % 128
                    v = pltpu.roll(v, shift, 1) if shift else v
                    acc = v if acc is None else jnp.where(lane >= SLOT * j, v, acc)
                ps[side, k] = acc
        if level == 2:
            for k in range(n // 2):
                rows_out[k] = e[h + k] + pltpu.roll(e[h + k + n // 2], 64, 1)
        index = 0
        pending = []
        for dt in range(-REACH[level], REACH[level] + 1):
            for dc in (-1, 0, 1):
                if not (dt or dc):
                    continue
                d = abs(dt)
                if dc == 0:
                    m = min(n, h - (d - 1) * n)
                    send_lo = h if dt < 0 else h + n - m
                    land = h + d * n if dt < 0 else h - (d - 1) * n - m
                    lanes = pl.ds(0, max(w, 128))
                    src = e.at[pl.ds(send_lo, m), :, lanes]
                    dst = e.at[pl.ds(land, m), :, lanes]
                    if level == 2 and d == 1:
                        src, dst = rows_out, rows_in.at[(1 - dt) // 2]
                else:
                    side = 0 if dc < 0 else 1
                    slot = (-dt + REACH[level]) * 2 + (1 if dc < 0 else 0)
                    if dt == 0:
                        src, dst = ps.at[side], pr.at[slot]
                    else:
                        k = 0 if dt < 0 else npk - 1
                        src, dst = ps.at[side, pl.ds(k, 1)], pr.at[slot, pl.ds(0, 1)]
                c = pltpu.make_async_remote_copy(
                    src_ref=src, dst_ref=dst, send_sem=ss.at[level, index], recv_sem=rsem.at[level, index],
                    device_id=device(dt, dc), device_id_type=MESH)
                pending.append((c, exists(dt, dc), exists(-dt, -dc)))
                index += 1
        for c, to, _ in pending:
            pl.when(to)(c.start)
        if meanwhile is not None:
            meanwhile()
        for c, to, _ in pending:
            pl.when(to)(c.wait_send)
        for c, _, come in pending:
            pl.when(come)(c.wait_recv)
        if level == 2:
            for k in range(n // 2):
                for side in (0, 1):
                    row = k + h + (2 * side - 1) * n
                    both = rows_in[side, k]
                    e[row] = jnp.where(lane < w, both, 0.0)
                    e[row + n // 2] = jnp.where(lane < w, pltpu.roll(both, 64, 1), 0.0)
        roff = w % 128
        hb = wt - 128

        def put(row, dt, k, j):
            slot = (dt + REACH[level]) * 2
            from_left = pr[slot, k]
            from_right = pr[slot + 1, k]
            s1 = (128 - SLOT - SLOT * j) % 128
            s2 = (roff - SLOT * j) % 128
            from_left = pltpu.roll(from_left, s1, 1) if s1 else from_left
            from_right = pltpu.roll(from_right, s2, 1) if s2 else from_right
            own = e[row, :, hb:hb + 128] if roff else jnp.zeros((ND, 128), jnp.float32)
            inner = jnp.where((lane >= roff) & (lane < roff + SLOT), from_right, own)
            e[row, :, hb:hb + 128] = jnp.where(lane >= 128 - SLOT, from_left, inner)

        for r in range(n):
            put(h + r, 0, r // 8, r % 8)
        for d in range(1, REACH[level] + 1):
            m = min(n, h - (d - 1) * n)
            for r in range(m):
                put(h - (d - 1) * n - m + r, -d, 0, (n - m + r) % 8)
                put(h + d * n + r, d, 0, r % 8)

    z = lax.broadcasted_iota(jnp.int32, (1, NZ, 1), 1)

    def diag_of(k_h, k_v):
        return 4.0 * k_h + k_v * jnp.where(z > 0, 2.0, 1.0)

    def coefs(e, r, count, scale):
        return scale * e[pl.ds(r, count), NZ:NZ + 1, :], e[pl.ds(r, count), NZ + 1:NZ + 2, :]

    def over(lo, hi, step, fn, block):
        if hi - lo <= block:
            for r in range(lo, hi, step):
                fn(r)
            return

        def loop(i, carry):
            for j in range(0, block, step):
                fn(lo + i * block + j)
            return carry
        lax.fori_loop(0, (hi - lo) // block, loop, 0)
        for r in range(lo + (hi - lo) // block * block, hi, step):
            fn(r)

    def block_of(e):
        return BLOCK[[x is e for x in es].index(True)]

    def first(e, rd, u, scale, lo, hi, lanes):
        def at(r, count=2):
            here, up = pl.ds(r, count), pl.ds(r + 1, count)
            k_h = scale * e[here, NZ:NZ + 1, lanes]
            k_v = e[here, NZ + 1:NZ + 2, lanes]
            diag = 4.0 * k_h + k_v * jnp.where(z[:, 0:8] > 0, 2.0, 1.0)
            inv = jnp.where(diag > 0.0, OMEGA / diag, 0.0)
            rd[here, :, lanes] = inv
            u[up, 0:8, lanes] = inv * e[here, 0:8, lanes]
            u[up, 8:16, lanes] = inv[:, 1:2] * e[here, 8:16, lanes]
        even = hi - (hi - lo) % 2
        over(lo, even, 2, at, block_of(e))
        if even < hi:
            at(even, 1)

    def terms(e, u, r, count, scale):
        wt = u.shape[2]
        k_h, k_v = coefs(e, r, count, scale)
        x = u[pl.ds(r + 1, count)]
        hs = u[pl.ds(r, count)] + u[pl.ds(r + 2, count)]
        hs = hs + pltpu.roll(x, 1, 2) + pltpu.roll(x, wt - 1, 2)
        vs = jnp.where(z < NZ - 1, pltpu.roll(x, NZ - 1, 1), 0.0) + jnp.where(z > 0, pltpu.roll(x, 1, 1), 0.0)
        return x, e[pl.ds(r, count), 0:NZ, :] + k_h * hs + k_v * vs, k_h, k_v

    def sweep(e, rd, u, v, scale, rows, cut=0):
        def at(r):
            x, t, _, _ = terms(e, u, r, 2, scale)
            x = (1.0 - OMEGA) * x
            v[pl.ds(r + 1, 2), 0:8] = x[:, 0:8] + rd[pl.ds(r, 2)] * t[:, 0:8]
            v[pl.ds(r + 1, 2), 8:16] = x[:, 8:16] + rd[pl.ds(r, 2), 1:2] * t[:, 8:16]
        over(cut, rows - cut, 2, at, block_of(e))

    def residue(e, u, r, count, scale):
        x, t, k_h, k_v = terms(e, u, r, count, scale)
        return t - diag_of(k_h, k_v) * x

    def restrict(level, u, t):
        e, h, n, w = es[level], HALO[level], sizes[level], widths[level]
        scale = 0.25 ** level
        wt = t.shape[2]

        def at(k):
            r = h + 2 * k
            both = residue(e, u, r, 2, scale)[:, :, 0:wt]
            t[k, 0:NZ] = 0.25 * (both[0] + both[1])
            t[k, NZ:ND] = 0.25 * (e[r, NZ:ND, 0:wt] + e[r + 1, NZ:ND, 0:wt])
        over(0, n // 2, 1, at, 4)
        out = dot2(t[...].reshape(n // 2 * ND, wt), down_matrix(wt, 128))
        if w // 2 < 128:
            out = jnp.where(lane < w // 2, out, 0.0)
        es[level + 1][pl.ds(HALO[level + 1], n // 2), :, 0:128] = out.reshape(n // 2, ND, 128)

    def prolong(level, u, lo, count, fine, fine_lo):
        wt, wf = u.shape[2], fine.shape[2]
        m = up_matrix(wt, wf, widths[level - 1])
        rows = dot2(u[lo + 1:lo + 1 + count].reshape(count * NZ, wt), m).reshape(count, NZ, wf)
        for k in range(count):
            for j in range(2):
                f = fine_lo + 1 + 2 * k + j
                fine[f] = fine[f] + rows[k]

    n0, n1, n2 = (sizes[k] + 2 * HALO[k] for k in range(3))
    def own(level, e, rd, u):
        h, n, w = HALO[level], sizes[level], widths[level]
        first(e, rd, u, 0.25 ** level, h, h + n, slice(0, w))

    def rest(level, e, rd, u):
        h, n, w, wt = HALO[level], sizes[level], widths[level], e.shape[2]
        first(e, rd, u, 0.25 ** level, 0, h, slice(0, wt))
        first(e, rd, u, 0.25 ** level, h, h + n, slice(w, wt))
        first(e, rd, u, 0.25 ** level, h + n, 2 * h + n, slice(0, wt))

    exchange(0, lambda: own(0, e0, rd0, ua0))
    rest(0, e0, rd0, ua0)
    sweep(e0, rd0, ua0, ub0, 1.0, n0, 1)
    restrict(0, ub0, t0)
    exchange(1, lambda: own(1, e1, rd1, ua1))
    rest(1, e1, rd1, ua1)
    sweep(e1, rd1, ua1, ub1, 0.25, n1, 1)
    restrict(1, ub1, t1)
    exchange(2)
    first(e2, rd2, ua2, 0.0625, 0, n2, slice(0, 128))
    for k in range(3):
        sweep(e2, rd2, ua2, ub2, 0.0625, n2, 2 * k + 1)
        sweep(e2, rd2, ub2, ua2, 0.0625, n2, 2 * k + 2)
    sweep(e2, rd2, ua2, ub2, 0.0625, n2, 7)
    prolong(2, ub2, HALO[2] - 2, sizes[2] + 4, ub1, HALO[1] - 4)
    sweep(e1, rd1, ub1, ua1, 0.25, n1, 2)
    sweep(e1, rd1, ua1, ub1, 0.25, n1, 3)
    prolong(1, ub1, HALO[1] - 2, sizes[1] + 4, ub0, 0)
    sweep(e0, rd0, ub0, ua0, 1.0, n0, 2)
    sweep(e0, rd0, ua0, ub0, 1.0, n0, 3)

    store = pltpu.make_async_copy(ub0.at[pl.ds(h0 + 1, nx), :, pl.ds(0, ny)], pot, in_sem.at[6])
    store.start()

    def last(k):
        rfine[pl.ds(k, 2)] = residue(e0, ub0, h0 + k, 2, 1.0)[:, :, 0:ny]
    over(0, nx, 2, last, 8)
    final = pltpu.make_async_copy(rfine, res, in_sem.at[7])
    final.start()
    store.wait()
    final.wait()


def hand_over(a, b, c, d, held, turned, in_sem, out_sem):
    steps = []
    for j, (src, dst) in enumerate(((a, c), (b, d))):
        for k in range(src.shape[0] // 8):
            i, rows = len(steps), pl.ds(8 * k, 8)
            come = pltpu.make_async_copy(src.at[rows], held.at[i], in_sem.at[i])
            go = pltpu.make_async_copy(turned.at[i], dst.at[:, rows, :], out_sem.at[i])
            come.start()
            steps.append((come, go))
    for i, (come, go) in enumerate(steps):
        come.wait()
        turned[i] = jnp.swapaxes(held[i], 0, 1)
        go.start()
    for _, go in steps:
        go.wait()


def solution(mesh):
    tiles, strips, subs = mesh.shape["tile"], mesh.shape["strip"], mesh.shape["sub"]

    def body(right_side, horiz_coef, vert_coef, panel_owner, panel_cell, panel_pressure):
        nz, nx, ny = right_side.shape
        rows = [n + 2 * h for n, h in zip((nx, nx // 2, nx // 4), HALO)]
        wts = (ny + 128, ny // 2 + 128, 128)
        f32 = jnp.float32
        scratch = [
            pltpu.VMEM((tiles, nx, ny), f32),
            pltpu.VMEM((max(tiles - 1, 1), nx, ny), f32),
            pltpu.VMEM((ND, nx, ny), f32),
        ]
        scratch += [pltpu.VMEM((rows[k], ND, wts[k]), f32) for k in range(3)]
        for k in range(3):
            scratch += [pltpu.VMEM((rows[k] + 2, NZ, wts[k]), f32)] * 2 + [pltpu.VMEM((rows[k], 8, wts[k]), f32)]
        scratch += [pltpu.VMEM((nx // 2, ND, ny), f32), pltpu.VMEM((nx // 4, ND, ny // 2), f32)]
        scratch += [pltpu.VMEM((nx, NZ, ny), f32)]
        scratch += [pltpu.VMEM((2, nx // 8 >> k, ND, 128), f32) for k in range(3)]
        scratch += [pltpu.VMEM((2 * (2 * REACH[k] + 1), nx // 8 >> k, ND, 128), f32) for k in range(3)]
        panels = panel_cell.shape[0]
        scratch += [pltpu.VMEM((panels // 128, 128), t) for t in (jnp.int32, jnp.int32, f32)]
        half = nx // 8
        scratch += [pltpu.VMEM((half, ND, 128), f32), pltpu.VMEM((2, half, ND, 128), f32)]
        scratch += [
            pltpu.SemaphoreType.DMA((max(tiles - 1, 1),)),
            pltpu.SemaphoreType.DMA((max(tiles - 1, 1),)),
            pltpu.SemaphoreType.DMA((3, 14)),
            pltpu.SemaphoreType.DMA((3, 14)),
            pltpu.SemaphoreType.DMA((8,)),
        ]
        out = jax.ShapeDtypeStruct((nz, nx, ny), f32)
        turned = jax.ShapeDtypeStruct((nx, nz, ny), f32)
        hbm = pl.BlockSpec(memory_space=pltpu.HBM)
        made = pl.pallas_call(
            functools.partial(kernel, (tiles, strips * subs, subs)),
            out_shape=(turned, turned),
            in_specs=[hbm] * 6,
            out_specs=(hbm, hbm),
            scratch_shapes=scratch,
            compiler_params=pltpu.CompilerParams(
                collective_id=0, has_side_effects=True, vmem_limit_bytes=VMEM_BYTES
            ),
        )(
            right_side, horiz_coef, vert_coef,
            panel_owner.reshape(panels // 128, 128), panel_cell.reshape(panels // 128, 128),
            panel_pressure.reshape(panels // 128, 128),
        )
        return pl.pallas_call(
            hand_over,
            out_shape=(out, out),
            in_specs=[hbm] * 2,
            out_specs=(hbm, hbm),
            scratch_shapes=[
                pltpu.VMEM((nx // 4, 8, nz, ny), f32),
                pltpu.VMEM((nx // 4, nz, 8, ny), f32),
                pltpu.SemaphoreType.DMA((nx // 4,)),
                pltpu.SemaphoreType.DMA((nx // 4,)),
            ],
            compiler_params=pltpu.CompilerParams(vmem_limit_bytes=VMEM_BYTES),
        )(*made)

    return jax.shard_map(
        body,
        mesh=mesh,
        in_specs=(
            P("group", "tile", ("strip", "sub")),
            P(("group", "tile"), ("strip", "sub")),
            P(("group", "tile"), ("strip", "sub")),
            P(("group", "tile", "strip", "sub"), None),
            P(("group", "tile", "strip", "sub")),
            P(("group", "tile", "strip", "sub")),
        ),
        out_specs=(P("group", "tile", ("strip", "sub")), P("group", "tile", ("strip", "sub"))),
        check_vma=False,
    )
```
